512 devices in a mesh: dom: 128 (over y, z, core), feat: 4 (over x).
Axes of the slice: x: 4, y: 8, z: 8, core: 2. Of those that a mesh axis runs over, the one named last changes fastest.
Arguments:
- features: bfloat16 [32768, 768], P('dom', 'feat'), may hold values from -6 to 6
- pre_act: bfloat16 [32768, 256], P('dom'), may hold values from -6 to 6
- out_grad: bfloat16 [32768, 256], P('dom', 'feat'), may hold values from -0.03125 to 0.03125
- w_second: bfloat16 [256, 256], P(None, 'feat'), may hold values from -0.375 to 0.375
- adj_tiles: int32 [256, 6, 128, 128], P('dom'), may hold values from 0 to 3, as said below
- tile_cols: int32 [256, 6], P('dom'), may hold values from 0 to 3, as said below
- tile_live: int32 [256], P('dom'), may hold values from 1 to 6, as said below
- halo_counts: int32 [16384], P('dom'), may hold values from 0 to 2, as said below
- border_rows: int32 [16384, 2], P('dom'), may hold values from 0 to 255
Outputs:
- grad_first: float32 [768, 256], P('feat')
- grad_second: float32 [256, 256], P(None, 'feat')
The draws below stay inside these ranges and needn't reach their ends.
Inputs may be any that keep to these rules, and one draw needn't show every extreme that they name: `adj_tiles`: entries are edge counts; every diagonal entry of slot 0 is at least 1. `tile_cols`: column blocks count the 2 own blocks first, then the boundary slots; slot 0 of a partition's row block b is its own block b. `tile_live`: every partition has a row block with all 6 slots live. `halo_counts`: entry p * 128 + p is 0; every partition keeps exactly 2 live slots for some peer.
All inputs are finite; a program needn't handle non-finite values.
Results may differ from the reference program's by a relative error of at most 0.0085.
Values may be sent and summed in bfloat16 or wider, within the bound.
A program may use at most 64 MiB of HBM per device.

```python
import jax
import jax.numpy as jnp
from jax import lax

F = 768
HID = 256
OUT = 256
ROWS = 256
HALO = 256
TILE = 128
SLOTS = 6
CAP = 2
NODES = 32768
BLOCKS = 256
PAIRS = 16384
N_DOM = 128


def draw_adj_tiles(key, part):
    key = jax.random.fold_in(key, 11)
    raw_draw = jax.random.randint(key, (BLOCKS, SLOTS, TILE, TILE), 0, 64)
    counts = jnp.where(raw_draw < 2, raw_draw + 1, 0)
    diagonal = (jnp.arange(TILE)[:, None] == jnp.arange(TILE)[None, :]).astype(jnp.int32)
    first_slot = (jnp.arange(SLOTS) == 0).astype(jnp.int32)
    self_loops = first_slot[:, None, None] * diagonal[None, :, :]
    return (counts + self_loops[None]).astype(jnp.int32)


def draw_tile_cols(key, part):
    key = jax.random.fold_in(key, 12)
    picked = jax.random.randint(key, (BLOCKS, SLOTS), 0, (ROWS + HALO) // TILE)
    own_block = jnp.arange(BLOCKS) % (ROWS // TILE)
    return jnp.where(jnp.arange(SLOTS)[None, :] == 0, own_block[:, None], picked).astype(jnp.int32)


def draw_tile_live(key, part):
    key = jax.random.fold_in(key, 13)
    first_key, second_key = jax.random.split(key)
    counts = jax.random.randint(first_key, (N_DOM, ROWS // TILE), 1, SLOTS + 1)
    chosen = jax.random.randint(second_key, (N_DOM, 1), 0, ROWS // TILE)
    counts = jnp.where(jnp.arange(ROWS // TILE)[None, :] == chosen, SLOTS, counts)
    return counts.reshape(BLOCKS).astype(jnp.int32)


def draw_halo_counts(key, part):
    key = jax.random.fold_in(key, 14)
    first_key, second_key = jax.random.split(key)
    counts = jax.random.randint(first_key, (N_DOM, N_DOM), 0, CAP + 1)
    offset = jax.random.randint(second_key, (N_DOM, 1), 1, N_DOM)
    row_ids = jnp.arange(N_DOM)[:, None]
    peer_ids = jnp.arange(N_DOM)[None, :]
    counts = jnp.where(peer_ids == (row_ids + offset) % N_DOM, CAP, counts)
    counts = jnp.where(peer_ids == row_ids, 0, counts)
    return counts.reshape(PAIRS).astype(jnp.int32)


def with_ends(entries, key, low, top_value):
    index_at = [jax.random.randint(jax.random.fold_in(key, axis), (), 0, length) for axis, length in enumerate(entries.shape)]
    widest = entries.shape.index(max(entries.shape))
    next_to = index_at[:widest] + [(index_at[widest] + 1) % entries.shape[widest]] + index_at[widest + 1:]
    return entries.at[tuple(index_at)].set(low).at[tuple(next_to)].set(top_value)


def block_scale(rng, extent, pieces, least, top_value):
    factor_of, own = 1.0, jax.random.fold_in(rng, 6)
    for axis_at, parts in pieces:
        draws = jnp.exp(jax.random.uniform(jax.random.fold_in(own, axis_at), (parts,), jnp.float32, least / len(pieces), top_value / len(pieces)))
        factor_of = factor_of * jnp.repeat(draws, extent[axis_at] // parts).reshape([-1 if axis == axis_at else 1 for axis in range(len(extent))])
    return factor_of


def noise(key, shape, width, bound, cuts=(), kind=jnp.bfloat16):
    values = width * jax.random.normal(key, shape, jnp.float32)
    if cuts:
        values = values * block_scale(key, shape, cuts, -0.22, 0.18)
    return jnp.clip(values, -bound, bound).astype(kind)


def setup_inputs(seed: int = 0) -> dict:
    arg_keys = jax.random.split(jax.random.key(seed), 10)
    return {
        "features": noise(arg_keys[0], (NODES, F), 1.0, 6.0, ((0, 128), (1, 4))),
        "pre_act": noise(arg_keys[1], (NODES, HID), 1.0, 6.0, ((0, 128),)),
        "out_grad": noise(arg_keys[2], (NODES, OUT), NODES ** -0.5, 0.03125, ((0, 128), (1, 4))),
        "w_second": noise(arg_keys[3], (HID, OUT), HID ** -0.5, 0.375, ((1, 4),)),
        "adj_tiles": draw_adj_tiles(jax.random.fold_in(arg_keys[9], 71), 0),
        "tile_cols": draw_tile_cols(jax.random.fold_in(arg_keys[9], 71), 0),
        "tile_live": draw_tile_live(jax.random.fold_in(arg_keys[9], 71), 0),
        "halo_counts": draw_halo_counts(jax.random.fold_in(arg_keys[9], 71), 0),
        "border_rows": with_ends(jax.random.randint(arg_keys[8], (PAIRS, CAP), 0, ROWS), jax.random.fold_in(arg_keys[8], 1), 0, ROWS - 1).astype(jnp.int32),
    }


def rounded(values):
    return lax.optimization_barrier(values.astype(jnp.bfloat16)).astype(jnp.float32)


def masked_tiles(tile_vals, col_ids, live_vals, halo_flags):
    col_blocks = (ROWS + HALO) // TILE
    column_live = jnp.concatenate([jnp.ones((ROWS,), jnp.bool_), halo_flags]).reshape(col_blocks, TILE)
    slot_flags = jnp.arange(SLOTS)[None, :] < live_vals[:, None]
    kept_mask = column_live[col_ids] & slot_flags[:, :, None]
    return jnp.where(kept_mask[:, :, None, :], tile_vals, 0).astype(jnp.float32)


def aggregate(tile_vals, col_ids, extended):
    columns = extended.shape[1]
    blocks = extended.reshape(-1, TILE, columns)
    summed = jnp.einsum("bsij,bsjw->biw", tile_vals, blocks[col_ids], precision=lax.Precision.HIGHEST)
    return summed.reshape(ROWS, columns)


def transposed(tile_vals, col_ids, source):
    col_blocks = (ROWS + HALO) // TILE
    columns = source.shape[1]
    blocks = source.reshape(-1, TILE, columns)
    products = jnp.einsum("bsij,biw->bsjw", tile_vals, blocks, precision=lax.Precision.HIGHEST)
    one_hot = (col_ids[:, :, None] == jnp.arange(col_blocks)[None, None, :]).astype(jnp.float32)
    placed = jnp.einsum("bsc,bsjw->cjw", one_hot, products, precision=lax.Precision.HIGHEST)
    return placed.reshape(ROWS + HALO, columns)


def reference(features, pre_act, out_grad, w_second, adj_tiles, tile_cols, tile_live, halo_counts, border_rows):
    row_blocks = ROWS // TILE
    owner_rows = border_rows.reshape(N_DOM, N_DOM, CAP)
    offsets = (jnp.arange(N_DOM, dtype=jnp.int32) * ROWS).astype(jnp.int32)
    halo_index = (jnp.transpose(owner_rows, (1, 0, 2)) + offsets[None, :, None]).astype(jnp.int32).reshape(N_DOM, HALO)
    halo_flags = (jnp.arange(CAP)[None, None, :] < halo_counts.reshape(N_DOM, N_DOM)[:, :, None]).reshape(N_DOM, HALO)
    activated = jnp.maximum(pre_act, 0)
    feature_vals = features.astype(jnp.float32)
    back_rows = jnp.dot(out_grad, w_second.T, preferred_element_type=jnp.float32)
    tile_sets = adj_tiles.reshape(N_DOM, row_blocks, SLOTS, TILE, TILE)
    col_sets = tile_cols.reshape(N_DOM, row_blocks, SLOTS)
    live_sets = tile_live.reshape(N_DOM, row_blocks)

    def first_pass(which):
        tile_vals = masked_tiles(tile_sets[which], col_sets[which], live_sets[which], halo_flags[which])
        degree = jnp.sum(tile_vals, axis=(1, 3)).reshape(ROWS, 1)
        start = (which * ROWS).astype(jnp.int32)
        own_rows = lax.dynamic_slice_in_dim(activated, start, ROWS, 0)
        extended = jnp.concatenate([own_rows, activated[halo_index[which]]], axis=0).astype(jnp.float32)
        mixed_act = (aggregate(tile_vals, col_sets[which], extended) / degree).astype(jnp.bfloat16)
        grad_rows = lax.dynamic_slice_in_dim(out_grad, start, ROWS, 0)
        second_part = jnp.dot(mixed_act.T, grad_rows, preferred_element_type=jnp.float32)
        scaled = rounded(lax.dynamic_slice_in_dim(back_rows, start, ROWS, 0) / degree)
        spread = transposed(tile_vals, col_sets[which], scaled)
        return second_part, spread, degree

    second_parts, spreads, degrees = lax.map(first_pass, jnp.arange(N_DOM, dtype=jnp.int32))
    grad_second = jnp.sum(second_parts, axis=0)
    grad_act = spreads[:, :ROWS].reshape(NODES, HID)
    grad_act = grad_act.at[halo_index.reshape(-1)].add(spreads[:, ROWS:].reshape(N_DOM * HALO, HID))
    grad_pre = rounded(jnp.where(pre_act > 0, grad_act, 0.0))

    def second_pass(which):
        tile_vals = masked_tiles(tile_sets[which], col_sets[which], live_sets[which], halo_flags[which])
        start = (which * ROWS).astype(jnp.int32)
        own_rows = lax.dynamic_slice_in_dim(feature_vals, start, ROWS, 0)
        extended = jnp.concatenate([own_rows, feature_vals[halo_index[which]]], axis=0)
        mixed_in = aggregate(tile_vals, col_sets[which], extended) / degrees[which]
        grad_rows = lax.dynamic_slice_in_dim(grad_pre, start, ROWS, 0)
        return jnp.dot(mixed_in.T, grad_rows, precision=lax.Precision.HIGHEST, preferred_element_type=jnp.float32)

    grad_first = jnp.sum(lax.map(second_pass, jnp.arange(N_DOM, dtype=jnp.int32)), axis=0)
    return grad_first, grad_second
```

```python
import jax
import jax.numpy as jnp
from jax import lax
from jax.experimental import pallas as pl
from jax.experimental.pallas import tpu as pltpu
from jax.sharding import PartitionSpec as P

MESH = pl.DeviceIdType.MESH
BF16 = jnp.bfloat16
F32 = jnp.float32

NY = 8
NZC = 16
NZ = 8
NX = 4
PHASES = 12


def dot(a, b):
    return lax.dot_general(a, b, (((1,), (0,)), ((), ())), preferred_element_type=F32)


def dot_nt(a, b):
    return lax.dot_general(a, b, (((1,), (1,)), ((), ())), preferred_element_type=F32)


def rows_of(ref, start, size):
    return ref.at[pl.ds(pl.multiple_of(start, size), size)]


def kernel(
    ft_hbm, pa_hbm, gt_hbm, wt_hbm, adj_hbm, cols_ref, live_ref, hc_hbm, br_hbm,
    o1_ref, o2_ref,
    ft, pa, gt, wt, adj, hc, br,
    amat, s0, r0, t0, u0, s1, r1, t1, u1, wall, sall,
    q0s, q1s, q0, q1, w0, w1, v0, v1, f0, f1,
    load_sem, send_sem, recv_sem,
):
    dom = lax.axis_index("dom")
    feat = lax.axis_index("feat")
    y = dom // NZC
    zc = dom % NZC
    z = zc // 2
    core = dom % 2
    yc = y * 2 + core

    def dom_y(k):
        return ((y + k) % NY) * NZC + zc

    def dom_zc(k):
        return y * NZC + (zc + k) % NZC

    def dom_z(k):
        return y * NZC + ((z + k) % NZ) * 2 + core

    def dom_yc(k):
        other = (yc + k) % 16
        return (other // 2) * NZC + z * 2 + other % 2

    loads = []
    for i, (src, dst) in enumerate(
        [(br_hbm, br), (adj_hbm, adj), (ft_hbm, ft), (hc_hbm, hc), (gt_hbm, gt), (wt_hbm, wt), (pa_hbm, pa)]
    ):
        copy = pltpu.make_async_copy(src, dst, load_sem.at[i])
        copy.start()
        loads.append(copy)
    ld_br, ld_adj, ld_ft, ld_hc, ld_gt, ld_wt, ld_pa = loads

    barrier = pltpu.get_barrier_semaphore()

    def greet(d, f):
        pl.semaphore_signal(barrier, inc=1, device_id=(d, f), device_id_type=MESH)

    for k in range(1, NY):
        greet(dom_y(k), feat)
    for k in range(1, NZC):
        greet(dom_zc(k), feat)
    for k in range(1, NY):
        greet(((y + k) % NY) * NZC + z * 2 + (1 - core), feat)
    for k in range(1, NX):
        greet(dom, (feat + k) % NX)
    partners = (NY - 1) * 2 + (NZC - 1) + (NX - 1)

    def send(phase, k, src, dst, device):
        copy = pltpu.make_async_remote_copy(
            src_ref=src,
            dst_ref=dst,
            send_sem=send_sem.at[phase, k],
            recv_sem=recv_sem.at[phase, k],
            device_id=device,
            device_id_type=MESH,
        )
        copy.start()
        return copy

    def scatter_y(phase, src, dst, rows):
        copies = []
        for k in range(1, NY):
            copies.append(
                send(phase, k, rows_of(src, ((y + k) % NY) * rows, rows), rows_of(dst, y * rows, rows), (dom_y(k), feat))
            )
        rows_of(dst, y * rows, rows)[...] = rows_of(src, y * rows, rows)[...]
        return copies

    def scatter_zc(phase, src, dst, rows):
        copies = []
        for k in range(1, NZC):
            copies.append(
                send(phase, k, rows_of(src, ((zc + k) % NZC) * rows, rows), rows_of(dst, zc * rows, rows), (dom_zc(k), feat))
            )
        rows_of(dst, zc * rows, rows)[...] = rows_of(src, zc * rows, rows)[...]
        return copies

    def arrive(copies):
        for copy in copies:
            copy.wait_recv()

    n = 256
    rows_i = lax.broadcasted_iota(jnp.int32, (n, n), 0)
    lanes_i = lax.broadcasted_iota(jnp.int32, (n, n), 1)
    one_hot = lambda cond: jnp.where(cond, 1.0, 0.0).astype(BF16)
    eye = one_hot(rows_i == lanes_i)
    perm = one_hot(lanes_i == ((rows_i >> 1) & 7) * 32 + (rows_i >> 4) * 2 + (rows_i & 1))
    perm_t = one_hot(lanes_i == ((rows_i >> 1) & 15) * 16 + (rows_i >> 5) * 2 + (rows_i & 1))
    eye128 = one_hot(
        lax.broadcasted_iota(jnp.int32, (128, 128), 0) == lax.broadcasted_iota(jnp.int32, (128, 128), 1)
    )
    peer_i = lax.broadcasted_iota(jnp.int32, (128, n), 0)
    slot_i = lax.broadcasted_iota(jnp.int32, (128, n), 1)
    even = one_hot(slot_i == 2 * peer_i)
    odd = one_hot(slot_i == 2 * peer_i + 1)

    ld_br.wait()
    border = br[...].astype(F32).astype(BF16)
    slot_row = dot(jnp.broadcast_to(border[0:1], (16, 128)), even) + dot(
        jnp.broadcast_to(border[1:2], (16, 128)), odd
    )
    hot_t = one_hot(rows_i.astype(F32) == slot_row[0:1])
    hot = dot_nt(eye, hot_t).astype(BF16)
    hot_p = dot_nt(perm, hot_t).astype(BF16)

    ld_ft.wait()
    s0[...] = dot_nt(hot, ft[0:128]).astype(BF16)

    pl.semaphore_wait(barrier, partners)
    c_s0 = scatter_y(0, s0, r0, 32)
    ld_wt.wait()
    c_w = []
    for k in range(1, NX):
        c_w.append(send(4, k, wt, rows_of(wall, feat * 64, 64), (dom, (feat + k) % NX)))
    rows_of(wall, feat * 64, 64)[...] = wt[...]

    ld_hc.wait()
    counts = jnp.broadcast_to(hc[...].astype(F32).astype(BF16), (16, 128))
    slot_counts = dot(counts, even + odd)[0:1]
    parity = (lax.broadcasted_iota(jnp.int32, (1, n), 1) & 1).astype(F32)
    flags = jnp.where(parity < slot_counts, 1.0, 0.0)
    ld_adj.wait()
    for b in range(2):
        for cb in range(4):
            total = jnp.zeros((128, 128), jnp.int32)
            for s in range(6):
                keep = jnp.logical_and(cols_ref[b, s] == cb, s < live_ref[b])
                total = total + (adj[b, s] & jnp.where(keep, -1, 0))
            total = total.astype(F32)
            if cb >= 2:
                total = total * flags[:, (cb - 2) * 128 : (cb - 1) * 128]
            amat[b * 128 : (b + 1) * 128, cb * 128 : (cb + 1) * 128] = total.astype(BF16)
    degree = dot_nt(jnp.ones((16, 512), BF16), amat[...])[0:1]

    ld_gt.wait()
    scaled = gt[...].astype(F32) / degree
    high = scaled.astype(BF16)
    low = (scaled - high.astype(F32)).astype(BF16)
    spread = dot(jnp.concatenate([high, low], axis=0), amat[...])
    spread = spread[0:64] + spread[64:128]
    own_part = spread[:, 0:256]
    zeros64 = jnp.zeros((64, n), BF16)
    s1[...] = (
        dot_nt(hot_p, jnp.concatenate([ft[128:192], zeros64], axis=0))
        + dot_nt(perm, jnp.concatenate([zeros64, spread[:, 256:512].astype(BF16)], axis=0))
    ).astype(BF16)
    c_s1 = scatter_zc(2, s1, r1, 16)

    a_own = amat[:, 0:256]
    a_halo = amat[:, 256:512]

    arrive(c_s0)
    t0[...] = dot(perm, r0[...]).astype(BF16)
    c_u0 = scatter_zc(1, t0, u0, 16)

    a_halo_p = dot_nt(a_halo, perm).astype(BF16)
    mixed = dot_nt(ft[...], a_own)

    arrive(c_s1)
    t1[...] = dot(perm_t, r1[...]).astype(BF16)
    c_u1 = scatter_y(3, t1, u1, 32)

    ld_pa.wait()
    pre = pa[...].astype(F32)
    act = jnp.maximum(pre, 0.0).astype(BF16)
    mask_t = dot_nt(eye, one_hot(pre > 0.0))
    arrive(c_w)
    w_full = dot_nt(eye, wall[...]).astype(BF16)

    arrive(c_u1)
    x1 = dot_nt(eye128, u1[...]).astype(BF16)
    gathered = (own_part + dot(x1[64:128], hot)).astype(BF16)
    rows_of(sall, feat * 64, 64)[...] = gathered
    c_x = []
    for k in range(1, NX):
        c_x.append(
            send(5, k, rows_of(sall, feat * 64, 64), rows_of(sall, feat * 64, 64), (dom, (feat + k) % NX))
        )
    second = dot(gathered, act)

    arrive(c_u0)
    x0 = dot_nt(eye128, u0[...]).astype(BF16)
    mixed_low = (mixed[0:128] + dot_nt(x0, a_halo_p)) / degree
    mixed_top = (mixed[128:192] + dot_nt(x1[0:64], a_halo)) / degree
    mixed_in = jnp.concatenate([mixed_low.astype(BF16), mixed_top.astype(BF16)], axis=0)

    arrive(c_x)
    grad_act = dot(w_full, sall[...])
    grad_pre = jnp.where(mask_t > 0.5, grad_act, 0.0).astype(BF16)
    first = dot_nt(mixed_in, grad_pre)

    q0s[0:192] = first[:, 0:128].astype(BF16)
    q1s[0:192] = first[:, 128:256].astype(BF16)
    q0s[192:256] = second[:, 0:128].astype(BF16)
    q1s[192:256] = second[:, 128:256].astype(BF16)

    c_q0, c_q1 = [], []
    for k in range(1, 16):
        c_q0.append(
            send(6, k, rows_of(q0s, ((yc + k) % 16) * 16, 16), rows_of(q0, yc * 16, 16), (dom_yc(k), feat))
        )
        c_q1.append(
            send(7, k, rows_of(q1s, ((zc + k) % 16) * 16, 16), rows_of(q1, zc * 16, 16), (dom_zc(k), feat))
        )
    rows_of(q0, yc * 16, 16)[...] = rows_of(q0s, yc * 16, 16)[...]
    rows_of(q1, zc * 16, 16)[...] = rows_of(q1s, zc * 16, 16)[...]

    def total_of(ref, members):
        total = ref[0:16].astype(F32)
        for i in range(1, members):
            total = total + ref[i * 16 : (i + 1) * 16].astype(F32)
        return total.astype(BF16)

    arrive(c_q0)
    part0 = total_of(q0, 16)
    w0[...] = part0
    c_v0 = []
    for k in range(1, NZ):
        c_v0.append(send(8, k, w0, rows_of(v0, z * 16, 16), (dom_z(k), feat)))
    rows_of(v0, z * 16, 16)[...] = part0
    arrive(c_q1)
    part1 = total_of(q1, 16)
    w1[...] = part1
    c_v1 = []
    for k in range(1, NY):
        c_v1.append(send(9, k, w1, rows_of(v1, y * 16, 16), (dom_y(k), feat)))
    rows_of(v1, y * 16, 16)[...] = part1

    arrive(c_v0)
    rows_of(f0, yc * 16, 16)[...] = total_of(v0, 8)
    c_f0 = []
    for k in range(1, 16):
        c_f0.append(
            send(10, k, rows_of(f0, yc * 16, 16), rows_of(f0, yc * 16, 16), (dom_yc(k), feat))
        )
    arrive(c_v1)
    rows_of(f1, zc * 16, 16)[...] = total_of(v1, 8)
    c_f1 = []
    for k in range(1, 16):
        c_f1.append(
            send(11, k, rows_of(f1, zc * 16, 16), rows_of(f1, zc * 16, 16), (dom_zc(k), feat))
        )
    arrive(c_f0)
    o1_ref[:, 0:128] = f0[0:192].astype(F32)
    o2_ref[:, 0:128] = f0[192:256].astype(F32)
    arrive(c_f1)
    o1_ref[:, 128:256] = f1[0:192].astype(F32)
    o2_ref[:, 128:256] = f1[192:256].astype(F32)

    for copies in (c_s0, c_w, c_s1, c_u0, c_u1, c_x, c_q0, c_q1, c_v0, c_v1, c_f0, c_f1):
        for copy in copies:
            copy.wait_send()


def body(
    features, pre_act, out_grad, w_second, adj_tiles, tile_cols, tile_live, halo_counts, border_rows
):
    anywhere = pl.BlockSpec(memory_space=pl.ANY)
    smem = pl.BlockSpec(memory_space=pltpu.SMEM)
    vmem = pl.BlockSpec(memory_space=pltpu.VMEM)
    half = pltpu.VMEM((256, 128), BF16)
    square = pltpu.VMEM((256, 256), BF16)
    grad_first, grad_second_t = pl.pallas_call(
        kernel,
        out_shape=(
            jax.ShapeDtypeStruct((192, 256), F32),
            jax.ShapeDtypeStruct((64, 256), F32),
        ),
        in_specs=[anywhere, anywhere, anywhere, anywhere, anywhere, smem, smem, anywhere, anywhere],
        out_specs=(vmem, vmem),
        scratch_shapes=[
            pltpu.VMEM((192, 256), BF16),
            square,
            pltpu.VMEM((64, 256), BF16),
            pltpu.VMEM((64, 256), BF16),
            pltpu.VMEM((2, 6, 128, 128), jnp.int32),
            pltpu.VMEM((1, 128), jnp.int32),
            pltpu.VMEM((2, 128), jnp.int32),
            pltpu.VMEM((256, 512), BF16),
            half, half, half, half, half, half, half, half,
            square, square,
            half, half, half, half,
            pltpu.VMEM((16, 128), BF16),
            pltpu.VMEM((16, 128), BF16),
            pltpu.VMEM((128, 128), BF16),
            pltpu.VMEM((128, 128), BF16),
            half, half,
            pltpu.SemaphoreType.DMA((7,)),
            pltpu.SemaphoreType.DMA((PHASES, 16)),
            pltpu.SemaphoreType.DMA((PHASES, 16)),
        ],
        compiler_params=pltpu.CompilerParams(collective_id=0, has_side_effects=True),
        name="sage_backward",
    )(
        features.T, pre_act, out_grad.T, w_second.T, adj_tiles, tile_cols, tile_live,
        halo_counts.reshape(1, 128), border_rows.T,
    )
    return grad_first, grad_second_t.T


def solution(mesh):
    in_specs = (
        P("dom", "feat"),
        P("dom", None),
        P("dom", "feat"),
        P(None, "feat"),
        P("dom", None, None, None),
        P("dom", None),
        P("dom"),
        P("dom"),
        P("dom", None),
    )
    out_specs = (P("feat", None), P(None, "feat"))
    return jax.shard_map(body, mesh=mesh, in_specs=in_specs, out_specs=out_specs, check_vma=False)
```

```python
import jax
import jax.numpy as jnp
from jax import lax
from jax.experimental import pallas as pl
from jax.experimental.pallas import tpu as pltpu
from jax.sharding import PartitionSpec as P

MESH = pl.DeviceIdType.MESH
BF16 = jnp.bfloat16
F32 = jnp.float32

NY = 8
NZC = 16
NZ = 8
NX = 4
PHASES = 12
FAR_8 = (4, 3, 5, 2, 6, 1, 7)
FAR_16 = (8, 7, 9, 6, 10, 5, 11, 4, 12, 3, 13, 2, 14, 1, 15)
FAR_4 = (2, 1, 3)


def dot(a, b):
    return lax.dot_general(a, b, (((1,), (0,)), ((), ())), preferred_element_type=F32)


def dot_nt(a, b):
    return lax.dot_general(a, b, (((1,), (1,)), ((), ())), preferred_element_type=F32)


def rows_of(ref, start, size):
    return ref.at[pl.ds(pl.multiple_of(start, size), size)]


def kernel(
    ft_hbm, pa_hbm, gt_hbm, wt_hbm, adj_hbm, cols_ref, live_ref, hc_hbm, br_hbm,
    out_ref,
    ft, pa, gt, wt, adj, hc, br,
    amat, s0, r0, t0, u0, s1, r1, t1, u1, wall, sall,
    q0s, q1s, q0, q1, w0, w1, v0, v1, f0, f1,
    load_sem, send_sem, recv_sem,
):
    dom = lax.axis_index("dom")
    feat = lax.axis_index("feat")
    y = dom // NZC
    zc = dom % NZC
    z = zc // 2
    core = dom % 2
    yc = y * 2 + core

    def dom_y(k):
        return ((y + k) % NY) * NZC + zc

    def dom_zc(k):
        return y * NZC + (zc + k) % NZC

    def dom_z(k):
        return y * NZC + ((z + k) % NZ) * 2 + core

    def dom_yc(k):
        other = (yc + k) % 16
        return (other // 2) * NZC + z * 2 + other % 2

    loads = []
    for i, (src, dst) in enumerate(
        [(br_hbm, br), (adj_hbm, adj), (ft_hbm, ft), (hc_hbm, hc), (gt_hbm, gt), (wt_hbm, wt), (pa_hbm, pa)]
    ):
        copy = pltpu.make_async_copy(src, dst, load_sem.at[i])
        copy.start()
        loads.append(copy)
    ld_br, ld_adj, ld_ft, ld_hc, ld_gt, ld_wt, ld_pa = loads

    barrier = pltpu.get_barrier_semaphore()

    def greet(d, f):
        pl.semaphore_signal(barrier, inc=1, device_id=(d, f), device_id_type=MESH)

    for k in range(1, NY):
        greet(dom_y(k), feat)
    for k in range(1, NZC):
        greet(dom_zc(k), feat)
    for k in range(1, NY):
        greet(((y + k) % NY) * NZC + z * 2 + (1 - core), feat)
    for k in range(1, NX):
        greet(dom, (feat + k) % NX)
    partners = (NY - 1) * 2 + (NZC - 1) + (NX - 1)

    def send(phase, src, dst, device):
        copy = pltpu.make_async_remote_copy(
            src_ref=src,
            dst_ref=dst,
            send_sem=send_sem.at[phase],
            recv_sem=recv_sem.at[phase],
            device_id=device,
            device_id_type=MESH,
        )
        copy.start()

    def scatter_y(phase, src, dst, rows):
        for k in FAR_8:
            send(phase, rows_of(src, ((y + k) % NY) * rows, rows), rows_of(dst, y * rows, rows), (dom_y(k), feat))
        rows_of(dst, y * rows, rows)[...] = rows_of(src, y * rows, rows)[...]

    def scatter_zc(phase, src, dst, rows):
        for k in FAR_16:
            send(phase, rows_of(src, ((zc + k) % NZC) * rows, rows), rows_of(dst, zc * rows, rows), (dom_zc(k), feat))
        rows_of(dst, zc * rows, rows)[...] = rows_of(src, zc * rows, rows)[...]

    def all_of(phase, ref, rows):
        return pltpu.make_async_remote_copy(
            src_ref=ref.at[pl.ds(0, rows)],
            dst_ref=ref.at[pl.ds(0, rows)],
            send_sem=send_sem.at[phase],
            recv_sem=recv_sem.at[phase],
            device_id=(dom_y(1), feat),
            device_id_type=MESH,
        )

    sent = []

    def arrive(phase, ref, rows):
        copies = all_of(phase, ref, rows)
        copies.wait_recv()
        sent.append(copies)

    n = 256
    rows_i = lax.broadcasted_iota(jnp.int32, (n, n), 0)
    lanes_i = lax.broadcasted_iota(jnp.int32, (n, n), 1)
    one_hot = lambda cond: jnp.where(cond, 1.0, 0.0).astype(BF16)
    eye = one_hot(rows_i == lanes_i)
    perm = one_hot(lanes_i == ((rows_i >> 1) & 7) * 32 + (rows_i >> 4) * 2 + (rows_i & 1))
    perm_t = one_hot(lanes_i == ((rows_i >> 1) & 15) * 16 + (rows_i >> 5) * 2 + (rows_i & 1))
    eye128 = one_hot(
        lax.broadcasted_iota(jnp.int32, (128, 128), 0) == lax.broadcasted_iota(jnp.int32, (128, 128), 1)
    )
    peer_i = lax.broadcasted_iota(jnp.int32, (128, n), 0)
    slot_i = lax.broadcasted_iota(jnp.int32, (128, n), 1)
    even = one_hot(slot_i == 2 * peer_i)
    odd = one_hot(slot_i == 2 * peer_i + 1)

    ld_br.wait()
    border = br[...].astype(F32).astype(BF16)
    slot_row = dot(jnp.broadcast_to(border[0:1], (16, 128)), even) + dot(
        jnp.broadcast_to(border[1:2], (16, 128)), odd
    )
    hot_t = one_hot(rows_i.astype(F32) == slot_row[0:1])
    hot = dot_nt(eye, hot_t).astype(BF16)
    hot_p = dot_nt(perm, hot_t).astype(BF16)

    ld_hc.wait()
    counts = jnp.broadcast_to(hc[...].astype(F32).astype(BF16), (16, 128))
    slot_counts = dot(counts, even + odd)[0:1]
    parity = (lax.broadcasted_iota(jnp.int32, (1, n), 1) & 1).astype(F32)
    flags = jnp.where(parity < slot_counts, 1.0, 0.0)
    ld_adj.wait()
    for b in range(2):
        for cb in range(4):
            total = jnp.zeros((128, 128), jnp.int32)
            for s in range(6):
                keep = jnp.logical_and(cols_ref[b, s] == cb, s < live_ref[b])
                total = total + (adj[b, s] & jnp.where(keep, -1, 0))
            total = total.astype(F32)
            if cb >= 2:
                total = total * flags[:, (cb - 2) * 128 : (cb - 1) * 128]
            amat[b * 128 : (b + 1) * 128, cb * 128 : (cb + 1) * 128] = total.astype(BF16)
    inverse = 1.0 / dot_nt(jnp.ones((16, 512), BF16), amat[...])[0:1]

    ld_gt.wait()
    scaled = gt[...].astype(F32) * inverse
    high = scaled.astype(BF16)
    low = (scaled - high.astype(F32)).astype(BF16)
    spread = dot(jnp.concatenate([high, low], axis=0), amat[...])
    spread = spread[0:64] + spread[64:128]
    own_part = spread[:, 0:256]
    zeros64 = jnp.zeros((64, n), BF16)
    ld_ft.wait()
    s1[...] = (
        dot_nt(hot_p, jnp.concatenate([ft[128:192], zeros64], axis=0))
        + dot_nt(perm, jnp.concatenate([zeros64, spread[:, 256:512].astype(BF16)], axis=0))
    ).astype(BF16)

    pl.semaphore_wait(barrier, partners)
    scatter_zc(2, s1, r1, 16)
    s0[...] = dot_nt(hot, ft[0:128]).astype(BF16)
    scatter_y(0, s0, r0, 32)
    ld_wt.wait()
    for k in FAR_4:
        send(4, wt, rows_of(wall, feat * 64, 64), (dom, (feat + k) % NX))
    rows_of(wall, feat * 64, 64)[...] = wt[...]

    a_own = amat[:, 0:256]
    a_halo = amat[:, 256:512]
    a_halo_p = dot_nt(a_halo, perm).astype(BF16)
    mixed = dot_nt(ft[...], a_own)
    ld_pa.wait()
    pre = pa[...].astype(F32)
    act = jnp.maximum(pre, 0.0).astype(BF16)
    mask_t = dot_nt(eye, one_hot(pre > 0.0))

    arrive(2, r1, 240)
    t1[...] = dot(perm_t, r1[...]).astype(BF16)
    scatter_y(3, t1, u1, 32)
    arrive(0, r0, 224)
    t0[...] = dot(perm, r0[...]).astype(BF16)
    scatter_zc(1, t0, u0, 16)

    arrive(4, wall, 192)
    w_full = dot_nt(eye, wall[...]).astype(BF16)

    arrive(3, u1, 224)
    x1 = dot_nt(eye128, u1[...]).astype(BF16)
    gathered = (own_part + dot(x1[64:128], hot)).astype(BF16)
    rows_of(sall, feat * 64, 64)[...] = gathered
    for k in FAR_4:
        send(5, rows_of(sall, feat * 64, 64), rows_of(sall, feat * 64, 64), (dom, (feat + k) % NX))
    second = dot(gathered, act)
    q0s[192:256] = second[:, 0:128].astype(BF16)
    q1s[192:256] = second[:, 128:256].astype(BF16)

    arrive(1, u0, 240)
    x0 = dot_nt(eye128, u0[...]).astype(BF16)
    mixed_low = (mixed[0:128] + dot_nt(x0, a_halo_p)) * inverse
    mixed_top = (mixed[128:192] + dot_nt(x1[0:64], a_halo)) * inverse
    mixed_in = jnp.concatenate([mixed_low.astype(BF16), mixed_top.astype(BF16)], axis=0)

    arrive(5, sall, 192)
    grad_act = dot(w_full, sall[...])
    grad_pre = jnp.where(mask_t > 0.5, grad_act, 0.0).astype(BF16)
    first = dot_nt(mixed_in, grad_pre)
    q0s[0:192] = first[:, 0:128].astype(BF16)
    q1s[0:192] = first[:, 128:256].astype(BF16)

    for k in FAR_16:
        send(6, rows_of(q0s, ((yc + k) % 16) * 16, 16), rows_of(q0, yc * 16, 16), (dom_yc(k), feat))
        send(7, rows_of(q1s, ((zc + k) % 16) * 16, 16), rows_of(q1, zc * 16, 16), (dom_zc(k), feat))
    rows_of(q0, yc * 16, 16)[...] = rows_of(q0s, yc * 16, 16)[...]
    rows_of(q1, zc * 16, 16)[...] = rows_of(q1s, zc * 16, 16)[...]

    def total_of(ref, members):
        total = ref[0:16].astype(F32)
        for i in range(1, members):
            total = total + ref[i * 16 : (i + 1) * 16].astype(F32)
        return total.astype(BF16)

    arrive(6, q0, 240)
    part0 = total_of(q0, 16)
    w0[...] = part0
    for k in FAR_8:
        send(8, w0, rows_of(v0, z * 16, 16), (dom_z(k), feat))
    rows_of(v0, z * 16, 16)[...] = part0
    arrive(7, q1, 240)
    part1 = total_of(q1, 16)
    w1[...] = part1
    for k in FAR_8:
        send(9, w1, rows_of(v1, y * 16, 16), (dom_y(k), feat))
    rows_of(v1, y * 16, 16)[...] = part1

    arrive(8, v0, 112)
    rows_of(f0, yc * 16, 16)[...] = total_of(v0, 8)
    for k in FAR_16:
        send(10, rows_of(f0, yc * 16, 16), rows_of(f0, yc * 16, 16), (dom_yc(k), feat))
    arrive(9, v1, 112)
    rows_of(f1, zc * 16, 16)[...] = total_of(v1, 8)
    for k in FAR_16:
        send(11, rows_of(f1, zc * 16, 16), rows_of(f1, zc * 16, 16), (dom_zc(k), feat))
    arrive(10, f0, 240)
    out_ref[:, 0:128] = f0[...]
    arrive(11, f1, 240)
    out_ref[:, 128:256] = f1[...]

    for copies in sent:
        copies.wait_send()


def body(
    features, pre_act, out_grad, w_second, adj_tiles, tile_cols, tile_live, halo_counts, border_rows
):
    anywhere = pl.BlockSpec(memory_space=pl.ANY)
    smem = pl.BlockSpec(memory_space=pltpu.SMEM)
    vmem = pl.BlockSpec(memory_space=pltpu.VMEM)
    half = pltpu.VMEM((256, 128), BF16)
    square = pltpu.VMEM((256, 256), BF16)
    grads = pl.pallas_call(
        kernel,
        out_shape=jax.ShapeDtypeStruct((256, 256), BF16),
        in_specs=[anywhere, anywhere, anywhere, anywhere, anywhere, smem, smem, anywhere, anywhere],
        out_specs=vmem,
        scratch_shapes=[
            pltpu.VMEM((192, 256), BF16),
            square,
            pltpu.VMEM((64, 256), BF16),
            pltpu.VMEM((64, 256), BF16),
            pltpu.VMEM((2, 6, 128, 128), jnp.int32),
            pltpu.VMEM((1, 128), jnp.int32),
            pltpu.VMEM((2, 128), jnp.int32),
            pltpu.VMEM((256, 512), BF16),
            half, half, half, half, half, half, half, half,
            square, square,
            half, half, half, half,
            pltpu.VMEM((16, 128), BF16),
            pltpu.VMEM((16, 128), BF16),
            pltpu.VMEM((128, 128), BF16),
            pltpu.VMEM((128, 128), BF16),
            half, half,
            pltpu.SemaphoreType.DMA((7,)),
            pltpu.SemaphoreType.DMA((PHASES,)),
            pltpu.SemaphoreType.DMA((PHASES,)),
        ],
        compiler_params=pltpu.CompilerParams(collective_id=0, has_side_effects=True),
        name="sage_backward",
    )(
        features.T, pre_act, out_grad.T, w_second.T, adj_tiles, tile_cols, tile_live,
        halo_counts.reshape(1, 128), border_rows.T,
    )
    return grads[0:192].astype(F32), grads[192:256].astype(F32).T


def solution(mesh):
    in_specs = (
        P("dom", "feat"),
        P("dom", None),
        P("dom", "feat"),
        P(None, "feat"),
        P("dom", None, None, None),
        P("dom", None),
        P("dom"),
        P("dom"),
        P("dom", None),
    )
    out_specs = (P("feat", None), P(None, "feat"))
    return jax.shard_map(body, mesh=mesh, in_specs=in_specs, out_specs=out_specs, check_vma=False)
```

```python
import jax
import jax.numpy as jnp
from jax import lax
from jax.experimental import pallas as pl
from jax.experimental.pallas import tpu as pltpu
from jax.sharding import PartitionSpec as P

MESH = pl.DeviceIdType.MESH
BF16 = jnp.bfloat16
F32 = jnp.float32

NY = 8
NZC = 16
NZ = 8
NX = 4
PHASES = 12
FAR_8 = (4, 3, 5, 2, 6, 1, 7)
FAR_16 = (8, 7, 9, 6, 10, 5, 11, 4, 12, 3, 13, 2, 14, 1, 15)
FAR_4 = (2, 1, 3)


def dot(a, b):
    return lax.dot_general(a, b, (((1,), (0,)), ((), ())), preferred_element_type=F32)


def dot_nt(a, b):
    return lax.dot_general(a, b, (((1,), (1,)), ((), ())), preferred_element_type=F32)


def rows_of(ref, start, size):
    return ref.at[pl.ds(pl.multiple_of(start, size), size)]


def kernel(
    ft_hbm, pa_hbm, gt_hbm, wt_hbm, adj_hbm, cols_hbm, live_hbm, hc_hbm, br_hbm,
    out_ref,
    ft, pa, gt, wt, adj, hc, br, cols_ref, live_ref,
    amat, s0, r0, t0, u0, s1, r1, t1, u1, wall, sall,
    q0s, q1s, q0, q1, w0, w1, v0, v1, f0, f1,
    load_sem, send_sem, recv_sem,
):
    dom = lax.axis_index("dom")
    feat = lax.axis_index("feat")
    y = dom // NZC
    zc = dom % NZC
    z = zc // 2
    core = dom % 2
    yc = y * 2 + core

    def dom_y(k):
        return ((y + k) % NY) * NZC + zc

    def dom_zc(k):
        return y * NZC + (zc + k) % NZC

    def dom_z(k):
        return y * NZC + ((z + k) % NZ) * 2 + core

    def dom_yc(k):
        other = (yc + k) % 16
        return (other // 2) * NZC + z * 2 + other % 2

    loads = []
    for i, (src, dst) in enumerate(
        [(br_hbm, br), (adj_hbm, adj), (ft_hbm, ft), (hc_hbm, hc), (gt_hbm, gt), (wt_hbm, wt), (pa_hbm, pa), (cols_hbm, cols_ref), (live_hbm, live_ref)]
    ):
        copy = pltpu.make_async_copy(src, dst, load_sem.at[i])
        copy.start()
        loads.append(copy)
    ld_br, ld_adj, ld_ft, ld_hc, ld_gt, ld_wt, ld_pa, ld_cols, ld_live = loads

    barrier = pltpu.get_barrier_semaphore()

    def greet(d, f):
        pl.semaphore_signal(barrier, inc=1, device_id=(d, f), device_id_type=MESH)

    for k in range(1, NY):
        greet(dom_y(k), feat)
    for k in range(1, NZC):
        greet(dom_zc(k), feat)
    for k in range(1, NY):
        greet(((y + k) % NY) * NZC + z * 2 + (1 - core), feat)
    for k in range(1, NX):
        greet(dom, (feat + k) % NX)
    partners = (NY - 1) * 2 + (NZC - 1) + (NX - 1)

    def send(phase, src, dst, device):
        copy = pltpu.make_async_remote_copy(
            src_ref=src,
            dst_ref=dst,
            send_sem=send_sem.at[phase],
            recv_sem=recv_sem.at[phase],
            device_id=device,
            device_id_type=MESH,
        )
        copy.start()

    def scatter_y(phase, src, dst, rows):
        for k in FAR_8:
            send(phase, rows_of(src, ((y + k) % NY) * rows, rows), rows_of(dst, y * rows, rows), (dom_y(k), feat))
        rows_of(dst, y * rows, rows)[...] = rows_of(src, y * rows, rows)[...]

    def scatter_zc(phase, src, dst, rows):
        for k in FAR_16:
            send(phase, rows_of(src, ((zc + k) % NZC) * rows, rows), rows_of(dst, zc * rows, rows), (dom_zc(k), feat))
        rows_of(dst, zc * rows, rows)[...] = rows_of(src, zc * rows, rows)[...]

    def all_of(phase, ref, rows):
        return pltpu.make_async_remote_copy(
            src_ref=ref.at[pl.ds(0, rows)],
            dst_ref=ref.at[pl.ds(0, rows)],
            send_sem=send_sem.at[phase],
            recv_sem=recv_sem.at[phase],
            device_id=(dom_y(1), feat),
            device_id_type=MESH,
        )

    sent = []

    def arrive(phase, ref, rows):
        copies = all_of(phase, ref, rows)
        copies.wait_recv()
        sent.append(copies)

    n = 256
    rows_i = lax.broadcasted_iota(jnp.int32, (n, n), 0)
    lanes_i = lax.broadcasted_iota(jnp.int32, (n, n), 1)
    one_hot = lambda cond: jnp.where(cond, 1.0, 0.0).astype(BF16)
    eye = one_hot(rows_i == lanes_i)
    perm = one_hot(lanes_i == ((rows_i >> 1) & 7) * 32 + (rows_i >> 4) * 2 + (rows_i & 1))
    perm_t = one_hot(lanes_i == ((rows_i >> 1) & 15) * 16 + (rows_i >> 5) * 2 + (rows_i & 1))
    eye128 = one_hot(
        lax.broadcasted_iota(jnp.int32, (128, 128), 0) == lax.broadcasted_iota(jnp.int32, (128, 128), 1)
    )
    peer_i = lax.broadcasted_iota(jnp.int32, (128, n), 0)
    slot_i = lax.broadcasted_iota(jnp.int32, (128, n), 1)
    even = one_hot(slot_i == 2 * peer_i)
    odd = one_hot(slot_i == 2 * peer_i + 1)

    ld_br.wait()
    border = br[...].astype(F32).astype(BF16)
    slot_row = dot(jnp.broadcast_to(border[0:1], (16, 128)), even) + dot(
        jnp.broadcast_to(border[1:2], (16, 128)), odd
    )
    hot_t = one_hot(rows_i.astype(F32) == slot_row[0:1])
    hot = dot_nt(eye, hot_t).astype(BF16)
    hot_p = dot_nt(perm, hot_t).astype(BF16)

    ld_hc.wait()
    counts = jnp.broadcast_to(hc[...].astype(F32).astype(BF16), (16, 128))
    slot_counts = dot(counts, even + odd)[0:1]
    parity = (lax.broadcasted_iota(jnp.int32, (1, n), 1) & 1).astype(F32)
    flags = jnp.where(parity < slot_counts, 1.0, 0.0)
    ld_cols.wait()
    ld_live.wait()
    ld_adj.wait()
    for b in range(2):
        for cb in range(4):
            total = jnp.zeros((128, 128), jnp.int32)
            for s in range(6):
                keep = jnp.logical_and(cols_ref[b, s] == cb, s < live_ref[b])
                total = total + (adj[b, s] & jnp.where(keep, -1, 0))
            total = total.astype(F32)
            if cb >= 2:
                total = total * flags[:, (cb - 2) * 128 : (cb - 1) * 128]
            amat[b * 128 : (b + 1) * 128, cb * 128 : (cb + 1) * 128] = total.astype(BF16)
    inverse = 1.0 / dot_nt(jnp.ones((16, 512), BF16), amat[...])[0:1]

    ld_gt.wait()
    scaled = gt[...].astype(F32) * inverse
    high = scaled.astype(BF16)
    low = (scaled - high.astype(F32)).astype(BF16)
    spread = dot(jnp.concatenate([high, low], axis=0), amat[...])
    spread = spread[0:64] + spread[64:128]
    own_part = spread[:, 0:256]
    zeros64 = jnp.zeros((64, n), BF16)
    ld_ft.wait()
    s1[...] = (
        dot_nt(hot_p, jnp.concatenate([ft[128:192], zeros64], axis=0))
        + dot_nt(perm, jnp.concatenate([zeros64, spread[:, 256:512].astype(BF16)], axis=0))
    ).astype(BF16)

    pl.semaphore_wait(barrier, partners)
    scatter_zc(2, s1, r1, 16)
    s0[...] = dot_nt(hot, ft[0:128]).astype(BF16)
    scatter_y(0, s0, r0, 32)
    ld_wt.wait()
    for k in FAR_4:
        send(4, wt, rows_of(wall, feat * 64, 64), (dom, (feat + k) % NX))
    rows_of(wall, feat * 64, 64)[...] = wt[...]

    a_own = amat[:, 0:256]
    a_halo = amat[:, 256:512]
    a_halo_p = dot_nt(a_halo, perm).astype(BF16)
    mixed = dot_nt(ft[...], a_own)
    ld_pa.wait()
    pre = pa[...].astype(F32)
    act = jnp.maximum(pre, 0.0).astype(BF16)
    mask_t = dot_nt(eye, one_hot(pre > 0.0))

    arrive(2, r1, 240)
    t1[...] = dot(perm_t, r1[...]).astype(BF16)
    scatter_y(3, t1, u1, 32)
    arrive(0, r0, 224)
    t0[...] = dot(perm, r0[...]).astype(BF16)
    scatter_zc(1, t0, u0, 16)

    arrive(4, wall, 192)
    w_full = dot_nt(eye, wall[...]).astype(BF16)

    arrive(3, u1, 224)
    x1 = dot_nt(eye128, u1[...]).astype(BF16)
    gathered = (own_part + dot(x1[64:128], hot)).astype(BF16)
    rows_of(sall, feat * 64, 64)[...] = gathered
    for k in FAR_4:
        send(5, rows_of(sall, feat * 64, 64), rows_of(sall, feat * 64, 64), (dom, (feat + k) % NX))
    second = dot(gathered, act)
    q0s[192:256] = second[:, 0:128].astype(BF16)
    q1s[192:256] = second[:, 128:256].astype(BF16)

    arrive(1, u0, 240)
    x0 = dot_nt(eye128, u0[...]).astype(BF16)
    mixed_low = (mixed[0:128] + dot_nt(x0, a_halo_p)) * inverse
    mixed_top = (mixed[128:192] + dot_nt(x1[0:64], a_halo)) * inverse
    mixed_in = jnp.concatenate([mixed_low.astype(BF16), mixed_top.astype(BF16)], axis=0)

    arrive(5, sall, 192)
    grad_act = dot(w_full, sall[...])
    grad_pre = jnp.where(mask_t > 0.5, grad_act, 0.0).astype(BF16)
    first = dot_nt(mixed_in, grad_pre)
    q0s[0:192] = first[:, 0:128].astype(BF16)
    q1s[0:192] = first[:, 128:256].astype(BF16)

    for k in FAR_16:
        send(6, rows_of(q0s, ((yc + k) % 16) * 16, 16), rows_of(q0, yc * 16, 16), (dom_yc(k), feat))
        send(7, rows_of(q1s, ((zc + k) % 16) * 16, 16), rows_of(q1, zc * 16, 16), (dom_zc(k), feat))
    rows_of(q0, yc * 16, 16)[...] = rows_of(q0s, yc * 16, 16)[...]
    rows_of(q1, zc * 16, 16)[...] = rows_of(q1s, zc * 16, 16)[...]

    def total_of(ref, members):
        total = ref[0:16].astype(F32)
        for i in range(1, members):
            total = total + ref[i * 16 : (i + 1) * 16].astype(F32)
        return total.astype(BF16)

    arrive(6, q0, 240)
    part0 = total_of(q0, 16)
    w0[...] = part0
    for k in FAR_8:
        send(8, w0, rows_of(v0, z * 16, 16), (dom_z(k), feat))
    rows_of(v0, z * 16, 16)[...] = part0
    arrive(7, q1, 240)
    part1 = total_of(q1, 16)
    w1[...] = part1
    for k in FAR_8:
        send(9, w1, rows_of(v1, y * 16, 16), (dom_y(k), feat))
    rows_of(v1, y * 16, 16)[...] = part1

    arrive(8, v0, 112)
    f0[...] = total_of(v0, 8)
    for k in FAR_16:
        send(10, f0, rows_of(out_ref, yc * 16, 16), (dom_yc(k), feat))
    own0 = pltpu.make_async_copy(f0, rows_of(out_ref, yc * 16, 16), load_sem.at[9])
    own0.start()
    arrive(9, v1, 112)
    f1[...] = total_of(v1, 8)
    for k in FAR_16:
        send(11, f1, rows_of(out_ref, 256 + zc * 16, 16), (dom_zc(k), feat))
    own1 = pltpu.make_async_copy(f1, rows_of(out_ref, 256 + zc * 16, 16), load_sem.at[10])
    own1.start()
    own0.wait()
    own1.wait()
    arrive(10, out_ref, 240)
    arrive(11, out_ref, 240)

    for copies in sent:
        copies.wait_send()


def widen(sums, first_ref, second_ref):
    for h in range(2):
        first_ref[:, h * 128 : (h + 1) * 128] = sums[h * 256 : h * 256 + 192].astype(F32)
        second_ref[:, h * 128 : (h + 1) * 128] = sums[h * 256 + 192 : h * 256 + 256].astype(F32)


def body(
    features, pre_act, out_grad, w_second, adj_tiles, tile_cols, tile_live, halo_counts, border_rows
):
    anywhere = pl.BlockSpec(memory_space=pl.ANY)
    vmem = pl.BlockSpec(memory_space=pltpu.VMEM)
    half = pltpu.VMEM((256, 128), BF16)
    square = pltpu.VMEM((256, 256), BF16)
    grads = pl.pallas_call(
        kernel,
        out_shape=pltpu.VMEM((512, 128), BF16),
        in_specs=[anywhere] * 9,
        out_specs=anywhere,
        scratch_shapes=[
            pltpu.VMEM((192, 256), BF16),
            square,
            pltpu.VMEM((64, 256), BF16),
            pltpu.VMEM((64, 256), BF16),
            pltpu.VMEM((2, 6, 128, 128), jnp.int32),
            pltpu.VMEM((1, 128), jnp.int32),
            pltpu.VMEM((2, 128), jnp.int32),
            pltpu.SMEM((2, 6), jnp.int32),
            pltpu.SMEM((2,), jnp.int32),
            pltpu.VMEM((256, 512), BF16),
            half, half, half, half, half, half, half, half,
            square, square,
            half, half, half, half,
            pltpu.VMEM((16, 128), BF16),
            pltpu.VMEM((16, 128), BF16),
            pltpu.VMEM((128, 128), BF16),
            pltpu.VMEM((128, 128), BF16),
            pltpu.VMEM((16, 128), BF16),
            pltpu.VMEM((16, 128), BF16),
            pltpu.SemaphoreType.DMA((11,)),
            pltpu.SemaphoreType.DMA((PHASES,)),
            pltpu.SemaphoreType.DMA((PHASES,)),
        ],
        compiler_params=pltpu.CompilerParams(collective_id=0, has_side_effects=True, vmem_limit_bytes=60 * 1024 * 1024),
        name="sage_backward",
    )(
        features.T, pre_act, out_grad.T, w_second.T, adj_tiles, tile_cols, tile_live,
        halo_counts.reshape(1, 128), border_rows.T,
    )
    grad_first, grad_second_t = pl.pallas_call(
        widen,
        out_shape=(
            jax.ShapeDtypeStruct((192, 256), F32),
            jax.ShapeDtypeStruct((64, 256), F32),
        ),
        in_specs=[vmem],
        out_specs=(vmem, vmem),
        compiler_params=pltpu.CompilerParams(vmem_limit_bytes=4 * 1024 * 1024),
        name="widen",
    )(grads)
    return grad_first, grad_second_t.T


def solution(mesh):
    in_specs = (
        P("dom", "feat"),
        P("dom", None),
        P("dom", "feat"),
        P(None, "feat"),
        P("dom", None, None, None),
        P("dom", None),
        P("dom"),
        P("dom"),
        P("dom", None),
    )
    out_specs = (P("feat", None), P(None, "feat"))
    return jax.shard_map(body, mesh=mesh, in_specs=in_specs, out_specs=out_specs, check_vma=False)
```

```python
import jax
import jax.numpy as jnp
from jax import lax
from jax.experimental import pallas as pl
from jax.experimental.pallas import tpu as pltpu
from jax.sharding import PartitionSpec as P

MESH = pl.DeviceIdType.MESH
BF16 = jnp.bfloat16
F32 = jnp.float32

NY = 8
NZC = 16
NZ = 8
NX = 4
PHASES = 13
FAR_8 = (4, 3, 5, 2, 6, 1, 7)
FAR_16 = (8, 7, 9, 6, 10, 5, 11, 4, 12, 3, 13, 2, 14, 1, 15)
FAR_4 = (2, 1, 3)


def dot(a, b):
    return lax.dot_general(a, b, (((1,), (0,)), ((), ())), preferred_element_type=F32)


def dot_nt(a, b):
    return lax.dot_general(a, b, (((1,), (1,)), ((), ())), preferred_element_type=F32)


def rows_of(ref, start, size):
    return ref.at[pl.ds(pl.multiple_of(start, size), size)]


def kernel(
    ft_hbm, pa_hbm, gt_hbm, wt_hbm, adj_hbm, cols_hbm, live_hbm, hc_hbm, br_hbm,
    out_ref,
    ft, pa, gt, wt, adj, hc, br, cols_ref, live_ref,
    amat, s0, r0, t0, u0, s1, r1, t1, u1, wall, sall, oall, t1s, su,
    q0s, q1s, q0, q1, w0, w1, v0, v1, f0, f1,
    load_sem, send_sem, recv_sem,
):
    dom = lax.axis_index("dom")
    feat = lax.axis_index("feat")
    y = dom // NZC
    zc = dom % NZC
    z = zc // 2
    core = dom % 2
    yc = y * 2 + core

    def dom_y(k):
        return ((y + k) % NY) * NZC + zc

    def dom_zc(k):
        return y * NZC + (zc + k) % NZC

    def dom_z(k):
        return y * NZC + ((z + k) % NZ) * 2 + core

    def place(j, own, size):
        return j + (j + size - own) // size

    def dom_yc(k):
        other = (yc + k) % 16
        return (other // 2) * NZC + z * 2 + other % 2

    barrier = pltpu.get_barrier_semaphore()

    def greet(d, f):
        pl.semaphore_signal(barrier, inc=1, device_id=(d, f), device_id_type=MESH)

    for k in FAR_16:
        greet(dom_zc(k), feat)
    for k in FAR_8:
        greet(dom_y(k), feat)
        greet(((y + k) % NY) * NZC + z * 2 + (1 - core), feat)
    for k in FAR_4:
        greet(dom, (feat + k) % NX)
    loads = []
    for i, (src, dst) in enumerate(
        [(br_hbm, br), (adj_hbm, adj), (ft_hbm, ft), (hc_hbm, hc), (gt_hbm, gt), (wt_hbm, wt), (pa_hbm, pa), (cols_hbm, cols_ref), (live_hbm, live_ref)]
    ):
        copy = pltpu.make_async_copy(src, dst, load_sem.at[i])
        copy.start()
        loads.append(copy)
    ld_br, ld_adj, ld_ft, ld_hc, ld_gt, ld_wt, ld_pa, ld_cols, ld_live = loads

    partners = (NY - 1) * 2 + (NZC - 1) + (NX - 1)

    def send(phase, src, dst, device):
        copy = pltpu.make_async_remote_copy(
            src_ref=src,
            dst_ref=dst,
            send_sem=send_sem.at[phase],
            recv_sem=recv_sem.at[phase],
            device_id=device,
            device_id_type=MESH,
        )
        copy.start()

    def scatter_y(phase, src, dst, rows):
        for k in FAR_8:
            send(phase, rows_of(src, ((y + k) % NY) * rows, rows), rows_of(dst, y * rows, rows), (dom_y(k), feat))
        rows_of(dst, y * rows, rows)[...] = rows_of(src, y * rows, rows)[...]

    def scatter_zc(phase, src, dst, rows):
        for k in FAR_16:
            send(phase, rows_of(src, ((zc + k) % NZC) * rows, rows), rows_of(dst, zc * rows, rows), (dom_zc(k), feat))
        rows_of(dst, zc * rows, rows)[...] = rows_of(src, zc * rows, rows)[...]

    def all_of(phase, ref, rows):
        return pltpu.make_async_remote_copy(
            src_ref=ref.at[pl.ds(0, rows)],
            dst_ref=ref.at[pl.ds(0, rows)],
            send_sem=send_sem.at[phase],
            recv_sem=recv_sem.at[phase],
            device_id=(dom_y(1), feat),
            device_id_type=MESH,
        )

    sent = []

    def arrive(phase, ref, rows):
        copies = all_of(phase, ref, rows)
        copies.wait_recv()
        sent.append(copies)

    n = 256
    rows_i = lax.broadcasted_iota(jnp.int32, (n, n), 0)
    lanes_i = lax.broadcasted_iota(jnp.int32, (n, n), 1)
    one_hot = lambda cond: jnp.where(cond, 1.0, 0.0).astype(BF16)
    eye = one_hot(rows_i == lanes_i)
    perm = one_hot(lanes_i == ((rows_i >> 1) & 7) * 32 + (rows_i >> 4) * 2 + (rows_i & 1))
    perm_t = one_hot(lanes_i == ((rows_i >> 1) & 15) * 16 + (rows_i >> 5) * 2 + (rows_i & 1))
    perm_p = one_hot(lanes_i == (rows_i & 15) * 16 + ((rows_i >> 4) & 7) * 2 + (rows_i >> 7))
    by_c = one_hot(lanes_i == (rows_i & 127) * 2 + (rows_i >> 7))
    eye128 = one_hot(
        lax.broadcasted_iota(jnp.int32, (128, 128), 0) == lax.broadcasted_iota(jnp.int32, (128, 128), 1)
    )
    peer_i = lax.broadcasted_iota(jnp.int32, (128, n), 0)
    slot_i = lax.broadcasted_iota(jnp.int32, (128, n), 1)
    even = one_hot(slot_i == 2 * peer_i)
    odd = one_hot(slot_i == 2 * peer_i + 1)

    ld_br.wait()
    border = br[...].astype(F32).astype(BF16)
    slot_row = dot(jnp.broadcast_to(border[0:1], (16, 128)), even) + dot(
        jnp.broadcast_to(border[1:2], (16, 128)), odd
    )
    hot_t = one_hot(rows_i.astype(F32) == slot_row[0:1])
    hot = dot_nt(eye, hot_t).astype(BF16)
    hot_p = dot_nt(perm, hot_t).astype(BF16)
    hot_c = dot_nt(by_c, hot_t).astype(BF16)

    ld_hc.wait()
    counts = jnp.broadcast_to(hc[...].astype(F32).astype(BF16), (16, 128))
    slot_counts = dot(counts, even + odd)[0:1]
    parity = (lax.broadcasted_iota(jnp.int32, (1, n), 1) & 1).astype(F32)
    flags = jnp.where(parity < slot_counts, 1.0, 0.0)
    ld_cols.wait()
    ld_live.wait()
    ld_adj.wait()
    for b in range(2):
        for cb in range(4):
            total = jnp.zeros((128, 128), jnp.int32)
            for s in range(6):
                keep = jnp.logical_and(cols_ref[b, s] == cb, s < live_ref[b])
                total = total + (adj[b, s] & jnp.where(keep, -1, 0))
            total = total.astype(F32)
            if cb >= 2:
                total = total * flags[:, (cb - 2) * 128 : (cb - 1) * 128]
            amat[b * 128 : (b + 1) * 128, cb * 128 : (cb + 1) * 128] = total.astype(BF16)
    inverse = 1.0 / dot_nt(jnp.ones((16, 512), BF16), amat[...])[0:1]

    ld_gt.wait()
    scaled = gt[...].astype(F32) * inverse
    high = scaled.astype(BF16)
    low = (scaled - high.astype(F32)).astype(BF16)
    spread = dot(jnp.concatenate([high, low], axis=0), amat[...])
    spread = spread[0:64] + spread[64:128]
    own_part = spread[:, 0:256]
    zeros64 = jnp.zeros((64, n), BF16)
    ld_ft.wait()
    s1[...] = (
        dot_nt(hot_p, jnp.concatenate([ft[128:192], zeros64], axis=0))
        + dot_nt(perm, jnp.concatenate([zeros64, spread[:, 256:512].astype(BF16)], axis=0))
    ).astype(BF16)

    pl.semaphore_wait(barrier, partners)
    scatter_zc(2, s1, r1, 16)
    s0[...] = dot_nt(hot, ft[0:128]).astype(BF16)
    scatter_y(0, s0, r0, 32)
    ld_wt.wait()
    for k in FAR_4:
        send(4, wt, rows_of(wall, feat * 64, 64), (dom, (feat + k) % NX))
    rows_of(wall, feat * 64, 64)[...] = wt[...]

    rows_of(oall, feat * 64, 64)[...] = own_part.astype(BF16)
    for k in FAR_4:
        send(5, rows_of(oall, feat * 64, 64), rows_of(oall, feat * 64, 64), (dom, (feat + k) % NX))

    a_own = amat[:, 0:256]
    a_halo = amat[:, 256:512]
    a_halo_p = dot_nt(a_halo, perm).astype(BF16)
    mixed = dot_nt(ft[...], a_own)
    ld_pa.wait()
    pre = pa[...].astype(F32)
    act = jnp.maximum(pre, 0.0).astype(BF16)
    mask_t = dot_nt(eye, one_hot(pre > 0.0))

    arrive(5, oall, 192)
    own_all = oall[...].astype(F32)
    arrive(4, wall, 192)
    w_full = dot_nt(eye, wall[...]).astype(BF16)

    arrive(2, r1, 240)
    arrive(0, r0, 224)
    packed = dot(perm_p, r1[...])
    t1s[...] = jnp.where(
        lax.broadcasted_iota(jnp.int32, (128, 128), 1) < 64, pltpu.roll(packed[0:128], 64, 1), packed[128:256]
    ).astype(BF16)
    for k in FAR_8 + (0,):
        for m in FAR_4 + (0,):
            if k + m > 0:
                send(
                    3,
                    rows_of(t1s, ((y + k) % NY) * 16, 16),
                    rows_of(su, feat * 128 + y * 16, 16),
                    (dom_y(k), (feat + m) % NX),
                )
    rows_of(su, feat * 128 + y * 16, 16)[...] = rows_of(t1s, y * 16, 16)[...]
    t0[...] = dot(perm, r0[...]).astype(BF16)
    scatter_zc(1, t0, u0, 16)
    t1[...] = dot(perm_t, r1[...]).astype(BF16)
    scatter_y(12, t1, u1, 32)

    arrive(3, su, 496)
    x_s = dot_nt(eye128, su[...]).astype(BF16)
    even_part = jnp.concatenate([x_s[0:64, i * 128 : (i + 1) * 128] for i in range(NX)], axis=0)
    odd_part = jnp.concatenate([x_s[64:128, i * 128 : (i + 1) * 128] for i in range(NX)], axis=0)
    gathered = own_all + dot(jnp.concatenate([even_part, odd_part], axis=1), hot_c)
    sall[...] = gathered.astype(BF16)

    arrive(1, u0, 240)
    x0 = dot_nt(eye128, u0[...]).astype(BF16)
    mixed_low = (mixed[0:128] + dot_nt(x0, a_halo_p)) * inverse
    arrive(12, u1, 224)
    x1 = dot_nt(eye128, u1[...]).astype(BF16)
    mixed_top = (mixed[128:192] + dot_nt(x1[0:64], a_halo)) * inverse
    mixed_in = jnp.concatenate([mixed_low.astype(BF16), mixed_top.astype(BF16)], axis=0)

    second = dot(rows_of(sall, feat * 64, 64)[...], act)
    q0s[192:256] = second[:, 0:128].astype(BF16)
    q1s[192:256] = second[:, 128:256].astype(BF16)
    grad_act = dot(w_full, sall[...])
    grad_pre = jnp.where(mask_t > 0.5, grad_act, 0.0).astype(BF16)
    first = dot_nt(mixed_in, grad_pre)
    q0s[0:192] = first[:, 0:128].astype(BF16)
    q1s[0:192] = first[:, 128:256].astype(BF16)

    for k in FAR_16:
        send(6, rows_of(q0s, ((yc + k) % 16) * 16, 16), rows_of(q0, yc * 16, 16), (dom_yc(k), feat))
        send(7, rows_of(q1s, ((zc + k) % 16) * 16, 16), rows_of(q1, zc * 16, 16), (dom_zc(k), feat))
    rows_of(q0, yc * 16, 16)[...] = rows_of(q0s, yc * 16, 16)[...]
    rows_of(q1, zc * 16, 16)[...] = rows_of(q1s, zc * 16, 16)[...]

    def total_of(ref, members):
        total = ref[0:16].astype(F32)
        for i in range(1, members):
            total = total + ref[i * 16 : (i + 1) * 16].astype(F32)
        return total.astype(BF16)

    arrive(6, q0, 240)
    part0 = total_of(q0, 16)
    w0[...] = part0
    for j in range(NZ - 1):
        send(8, w0, rows_of(v0, z * 16, 16), (y * NZC + place(j, z, NZ) * 2 + core, feat))
    rows_of(v0, z * 16, 16)[...] = part0
    arrive(7, q1, 240)
    part1 = total_of(q1, 16)
    w1[...] = part1
    for j in range(NY - 1):
        send(9, w1, rows_of(v1, y * 16, 16), (place(j, y, NY) * NZC + zc, feat))
    rows_of(v1, y * 16, 16)[...] = part1

    arrive(8, v0, 112)
    f0[...] = total_of(v0, 8)
    for j in range(15):
        to = place(j, y * 2 + 1 - core, 16)
        send(10, f0, rows_of(out_ref, yc * 16, 16), ((to // 2) * NZC + z * 2 + 1 - to % 2, feat))
    own0 = pltpu.make_async_copy(f0, rows_of(out_ref, yc * 16, 16), load_sem.at[9])
    own0.start()
    arrive(9, v1, 112)
    f1[...] = total_of(v1, 8)
    for j in range(15):
        to = place(j, z * 2 + 1 - core, 16)
        send(11, f1, rows_of(out_ref, 256 + zc * 16, 16), (y * NZC + (to // 2) * 2 + 1 - to % 2, feat))
    own1 = pltpu.make_async_copy(f1, rows_of(out_ref, 256 + zc * 16, 16), load_sem.at[10])
    own1.start()
    own0.wait()
    own1.wait()
    arrive(10, out_ref, 240)
    arrive(11, out_ref, 240)

    for copies in sent:
        copies.wait_send()


def widen(sums, first_ref, second_ref):
    for h in range(2):
        first_ref[:, h * 128 : (h + 1) * 128] = sums[h * 256 : h * 256 + 192].astype(F32)
        second_ref[:, h * 128 : (h + 1) * 128] = sums[h * 256 + 192 : h * 256 + 256].astype(F32)


def body(
    features, pre_act, out_grad, w_second, adj_tiles, tile_cols, tile_live, halo_counts, border_rows
):
    anywhere = pl.BlockSpec(memory_space=pl.ANY)
    vmem = pl.BlockSpec(memory_space=pltpu.VMEM)
    half = pltpu.VMEM((256, 128), BF16)
    square = pltpu.VMEM((256, 256), BF16)
    grads = pl.pallas_call(
        kernel,
        out_shape=pltpu.VMEM((512, 128), BF16),
        in_specs=[anywhere] * 9,
        out_specs=anywhere,
        scratch_shapes=[
            pltpu.VMEM((192, 256), BF16),
            square,
            pltpu.VMEM((64, 256), BF16),
            pltpu.VMEM((64, 256), BF16),
            pltpu.VMEM((2, 6, 128, 128), jnp.int32),
            pltpu.VMEM((1, 128), jnp.int32),
            pltpu.VMEM((2, 128), jnp.int32),
            pltpu.SMEM((2, 6), jnp.int32),
            pltpu.SMEM((2,), jnp.int32),
            pltpu.VMEM((256, 512), BF16),
            half, half, half, half, half, half, half, half,
            square, square, square,
            pltpu.VMEM((128, 128), BF16),
            pltpu.VMEM((512, 128), BF16),
            half, half, half, half,
            pltpu.VMEM((16, 128), BF16),
            pltpu.VMEM((16, 128), BF16),
            pltpu.VMEM((128, 128), BF16),
            pltpu.VMEM((128, 128), BF16),
            pltpu.VMEM((16, 128), BF16),
            pltpu.VMEM((16, 128), BF16),
            pltpu.SemaphoreType.DMA((11,)),
            pltpu.SemaphoreType.DMA((PHASES,)),
            pltpu.SemaphoreType.DMA((PHASES,)),
        ],
        compiler_params=pltpu.CompilerParams(collective_id=0, has_side_effects=True, vmem_limit_bytes=60 * 1024 * 1024),
        name="sage_backward",
    )(
        features.T, pre_act, out_grad.T, w_second.T, adj_tiles, tile_cols, tile_live,
        halo_counts.reshape(1, 128), border_rows.T,
    )
    grad_first, grad_second_t = pl.pallas_call(
        widen,
        out_shape=(
            jax.ShapeDtypeStruct((192, 256), F32),
            jax.ShapeDtypeStruct((64, 256), F32),
        ),
        in_specs=[vmem],
        out_specs=(vmem, vmem),
        compiler_params=pltpu.CompilerParams(vmem_limit_bytes=4 * 1024 * 1024),
        name="widen",
    )(grads)
    return grad_first, grad_second_t.T


def solution(mesh):
    in_specs = (
        P("dom", "feat"),
        P("dom", None),
        P("dom", "feat"),
        P(None, "feat"),
        P("dom", None, None, None),
        P("dom", None),
        P("dom"),
        P("dom"),
        P("dom", None),
    )
    out_specs = (P("feat", None), P(None, "feat"))
    return jax.shard_map(body, mesh=mesh, in_specs=in_specs, out_specs=out_specs, check_vma=False)
```

```python
import jax
import jax.numpy as jnp
from jax import lax
from jax.experimental import pallas as pl
from jax.experimental.pallas import tpu as pltpu
from jax.sharding import PartitionSpec as P

MESH = pl.DeviceIdType.MESH
BF16 = jnp.bfloat16
F32 = jnp.float32

NY = 8
NZC = 16
NZ = 8
NX = 4
PHASES = 12
FAR_8 = (4, 3, 5, 2, 6, 1, 7)
FAR_16 = (8, 7, 9, 6, 10, 5, 11, 4, 12, 3, 13, 2, 14, 1, 15)
FAR_4 = (2, 1, 3)


def dot(a, b):
    return lax.dot_general(a, b, (((1,), (0,)), ((), ())), preferred_element_type=F32)


def dot_nt(a, b):
    return lax.dot_general(a, b, (((1,), (1,)), ((), ())), preferred_element_type=F32)


def rows_of(ref, start, size):
    return ref.at[pl.ds(pl.multiple_of(start, size), size)]


def kernel(
    ft_hbm, pa_hbm, gt_hbm, wt_hbm, adj_hbm, cols_hbm, live_hbm, hc_hbm, br_hbm,
    out_ref,
    ft, pa, gt, wt, adj, hc, br, cols_ref, live_ref,
    amat, s0, r0, t0, u0, s1, r1, wall, sall, oall, t1s, su,
    q0s, q1s, q0, q1, w0, w1, v0, v1, f0, f1,
    load_sem, send_sem, recv_sem, ready_sem,
):
    dom = lax.axis_index("dom")
    feat = lax.axis_index("feat")
    y = dom // NZC
    zc = dom % NZC
    z = zc // 2
    core = dom % 2
    yc = y * 2 + core

    def dom_y(k):
        return ((y + k) % NY) * NZC + zc

    def dom_zc(k):
        return y * NZC + (zc + k) % NZC

    def dom_z(k):
        return y * NZC + ((z + k) % NZ) * 2 + core

    def place(j, own, size):
        return j + (j + size - own) // size

    def dom_yc(k):
        other = (yc + k) % 16
        return (other // 2) * NZC + z * 2 + other % 2

    barrier = pltpu.get_barrier_semaphore()

    def greet(d, f):
        pl.semaphore_signal(barrier, inc=1, device_id=(d, f), device_id_type=MESH)

    for k in FAR_16:
        greet(dom_zc(k), feat)
    for k in FAR_8:
        greet(dom_y(k), feat)
        greet(((y + k) % NY) * NZC + z * 2 + (1 - core), feat)
    for k in FAR_4:
        greet(dom, (feat + k) % NX)
    loads = []
    for i, (src, dst) in enumerate(
        [(br_hbm, br), (adj_hbm, adj), (ft_hbm, ft), (hc_hbm, hc), (gt_hbm, gt), (wt_hbm, wt), (pa_hbm, pa), (cols_hbm, cols_ref), (live_hbm, live_ref)]
    ):
        copy = pltpu.make_async_copy(src, dst, load_sem.at[i])
        copy.start()
        loads.append(copy)
    ld_br, ld_adj, ld_ft, ld_hc, ld_gt, ld_wt, ld_pa, ld_cols, ld_live = loads

    partners = (NY - 1) * 2 + (NZC - 1) + (NX - 1)

    def send(phase, src, dst, device):
        copy = pltpu.make_async_remote_copy(
            src_ref=src,
            dst_ref=dst,
            send_sem=send_sem.at[phase],
            recv_sem=recv_sem.at[phase],
            device_id=device,
            device_id_type=MESH,
        )
        copy.start()

    def scatter_y(phase, src, dst, rows):
        for k in FAR_8:
            send(phase, rows_of(src, ((y + k) % NY) * rows, rows), rows_of(dst, y * rows, rows), (dom_y(k), feat))
        rows_of(dst, y * rows, rows)[...] = rows_of(src, y * rows, rows)[...]

    def scatter_zc(phase, src, dst, rows):
        for k in FAR_16:
            send(phase, rows_of(src, ((zc + k) % NZC) * rows, rows), rows_of(dst, zc * rows, rows), (dom_zc(k), feat))
        rows_of(dst, zc * rows, rows)[...] = rows_of(src, zc * rows, rows)[...]

    def all_of(phase, ref, rows):
        return pltpu.make_async_remote_copy(
            src_ref=ref.at[pl.ds(0, rows)],
            dst_ref=ref.at[pl.ds(0, rows)],
            send_sem=send_sem.at[phase],
            recv_sem=recv_sem.at[phase],
            device_id=(dom_y(1), feat),
            device_id_type=MESH,
        )

    sent = []

    def arrive(phase, ref, rows):
        copies = all_of(phase, ref, rows)
        copies.wait_recv()
        sent.append(copies)

    n = 256
    rows_i = lax.broadcasted_iota(jnp.int32, (n, n), 0)
    lanes_i = lax.broadcasted_iota(jnp.int32, (n, n), 1)
    one_hot = lambda cond: jnp.where(cond, 1.0, 0.0).astype(BF16)
    eye = one_hot(rows_i == lanes_i)
    perm = one_hot(lanes_i == ((rows_i >> 1) & 7) * 32 + (rows_i >> 4) * 2 + (rows_i & 1))
    perm_p = one_hot(lanes_i == (rows_i & 15) * 16 + ((rows_i >> 4) & 7) * 2 + (rows_i >> 7))
    by_c = one_hot(lanes_i == (rows_i & 127) * 2 + (rows_i >> 7))
    eye128 = one_hot(
        lax.broadcasted_iota(jnp.int32, (128, 128), 0) == lax.broadcasted_iota(jnp.int32, (128, 128), 1)
    )
    peer_i = lax.broadcasted_iota(jnp.int32, (128, n), 0)
    slot_i = lax.broadcasted_iota(jnp.int32, (128, n), 1)
    even = one_hot(slot_i == 2 * peer_i)
    odd = one_hot(slot_i == 2 * peer_i + 1)

    ld_br.wait()
    border = br[...].astype(F32).astype(BF16)
    slot_row = dot(jnp.broadcast_to(border[0:1], (16, 128)), even) + dot(
        jnp.broadcast_to(border[1:2], (16, 128)), odd
    )
    hot_t = one_hot(rows_i.astype(F32) == slot_row[0:1])
    hot = dot_nt(eye, hot_t).astype(BF16)
    hot_c = dot_nt(by_c, hot_t).astype(BF16)

    ld_hc.wait()
    counts = jnp.broadcast_to(hc[...].astype(F32).astype(BF16), (16, 128))
    slot_counts = dot(counts, even + odd)[0:1]
    parity = (lax.broadcasted_iota(jnp.int32, (1, n), 1) & 1).astype(F32)
    flags = jnp.where(parity < slot_counts, 1.0, 0.0)
    ld_cols.wait()
    ld_live.wait()
    ld_adj.wait()
    for b in range(2):
        for cb in range(4):
            total = jnp.zeros((128, 128), jnp.int32)
            for s in range(6):
                keep = jnp.logical_and(cols_ref[b, s] == cb, s < live_ref[b])
                total = total + (adj[b, s] & jnp.where(keep, -1, 0))
            total = total.astype(F32)
            if cb >= 2:
                total = total * flags[:, (cb - 2) * 128 : (cb - 1) * 128]
            amat[b * 128 : (b + 1) * 128, cb * 128 : (cb + 1) * 128] = total.astype(BF16)
    inverse = 1.0 / dot_nt(jnp.ones((16, 512), BF16), amat[...])[0:1]

    ld_gt.wait()
    scaled = gt[...].astype(F32) * inverse
    high = scaled.astype(BF16)
    low = (scaled - high.astype(F32)).astype(BF16)
    spread = dot(jnp.concatenate([high, low], axis=0), amat[...])
    spread = spread[0:64] + spread[64:128]
    own_part = spread[:, 0:256]
    halo_part = spread[:, 256:512].astype(BF16)
    s1[...] = dot_nt(perm, jnp.concatenate([halo_part, halo_part], axis=0)).astype(BF16)

    pl.semaphore_wait(barrier, partners)
    for k in FAR_8:
        pl.semaphore_signal(ready_sem, inc=1, device_id=(dom_y(k), feat), device_id_type=MESH)
    scatter_zc(2, s1, r1, 16)
    ld_ft.wait()
    s0[...] = dot_nt(hot, jnp.concatenate([ft[...], jnp.zeros((64, n), BF16)], axis=0)).astype(BF16)
    scatter_y(0, s0, r0, 32)
    ld_wt.wait()
    for k in FAR_4:
        send(4, wt, rows_of(wall, feat * 64, 64), (dom, (feat + k) % NX))
    rows_of(wall, feat * 64, 64)[...] = wt[...]

    rows_of(oall, feat * 64, 64)[...] = own_part.astype(BF16)
    for k in FAR_4:
        send(5, rows_of(oall, feat * 64, 64), rows_of(oall, feat * 64, 64), (dom, (feat + k) % NX))

    a_own = amat[:, 0:256]
    a_halo = amat[:, 256:512]
    a_halo_p = dot_nt(a_halo, perm).astype(BF16)
    mixed = dot_nt(ft[...], a_own)
    ld_pa.wait()
    pre = pa[...].astype(F32)
    act = jnp.maximum(pre, 0.0).astype(BF16)
    mask_t = dot_nt(eye, one_hot(pre > 0.0))

    arrive(2, r1, 240)
    pl.semaphore_wait(ready_sem, NY - 1)
    packed = dot(perm_p, r1[...])
    t1s[...] = jnp.where(
        lax.broadcasted_iota(jnp.int32, (128, 128), 1) < 64, packed[0:128], packed[128:256]
    ).astype(BF16)
    for k in FAR_8 + (0,):
        for m in FAR_4 + (0,):
            if k + m > 0:
                send(
                    3,
                    rows_of(t1s, ((y + k) % NY) * 16, 16),
                    rows_of(su, feat * 128 + y * 16, 16),
                    (dom_y(k), (feat + m) % NX),
                )
    rows_of(su, feat * 128 + y * 16, 16)[...] = rows_of(t1s, y * 16, 16)[...]
    arrive(0, r0, 224)
    t0[...] = dot(perm, r0[...]).astype(BF16)
    scatter_zc(1, t0, u0, 16)

    arrive(5, oall, 192)
    own_all = oall[...].astype(F32)
    arrive(4, wall, 192)
    w_full = dot_nt(eye, wall[...]).astype(BF16)

    arrive(3, su, 496)
    x_s = dot_nt(eye128, su[...]).astype(BF16)
    even_part = jnp.concatenate([x_s[0:64, i * 128 : (i + 1) * 128] for i in range(NX)], axis=0)
    odd_part = jnp.concatenate([x_s[64:128, i * 128 : (i + 1) * 128] for i in range(NX)], axis=0)
    gathered = own_all + dot(jnp.concatenate([even_part, odd_part], axis=1), hot_c)
    sall[...] = gathered.astype(BF16)

    arrive(1, u0, 240)
    x0 = dot_nt(eye, u0[...]).astype(BF16)
    mixed_in = ((mixed + dot_nt(x0[0:192], a_halo_p)) * inverse).astype(BF16)

    second = dot(rows_of(sall, feat * 64, 64)[...], act)
    q0s[192:256] = second[:, 0:128].astype(BF16)
    q1s[192:256] = second[:, 128:256].astype(BF16)
    grad_act = dot(w_full, sall[...])
    grad_pre = jnp.where(mask_t > 0.5, grad_act, 0.0).astype(BF16)
    first = dot_nt(mixed_in, grad_pre)
    q0s[0:192] = first[:, 0:128].astype(BF16)
    q1s[0:192] = first[:, 128:256].astype(BF16)

    for k in FAR_16:
        send(6, rows_of(q0s, ((yc + k) % 16) * 16, 16), rows_of(q0, yc * 16, 16), (dom_yc(k), feat))
        send(7, rows_of(q1s, ((zc + k) % 16) * 16, 16), rows_of(q1, zc * 16, 16), (dom_zc(k), feat))
    rows_of(q0, yc * 16, 16)[...] = rows_of(q0s, yc * 16, 16)[...]
    rows_of(q1, zc * 16, 16)[...] = rows_of(q1s, zc * 16, 16)[...]

    def total_of(ref, members):
        total = ref[0:16].astype(F32)
        for i in range(1, members):
            total = total + ref[i * 16 : (i + 1) * 16].astype(F32)
        return total.astype(BF16)

    arrive(6, q0, 240)
    part0 = total_of(q0, 16)
    w0[...] = part0
    for j in range(NZ - 1):
        send(8, w0, rows_of(v0, z * 16, 16), (y * NZC + place(j, z, NZ) * 2 + core, feat))
    rows_of(v0, z * 16, 16)[...] = part0
    arrive(7, q1, 240)
    part1 = total_of(q1, 16)
    w1[...] = part1
    for j in range(NY - 1):
        send(9, w1, rows_of(v1, y * 16, 16), (place(j, y, NY) * NZC + zc, feat))
    rows_of(v1, y * 16, 16)[...] = part1

    arrive(8, v0, 112)
    f0[...] = total_of(v0, 8)
    for j in range(15):
        to = place(j, y * 2 + 1 - core, 16)
        send(10, f0, rows_of(out_ref, yc * 16, 16), ((to // 2) * NZC + z * 2 + 1 - to % 2, feat))
    own0 = pltpu.make_async_copy(f0, rows_of(out_ref, yc * 16, 16), load_sem.at[9])
    own0.start()
    arrive(9, v1, 112)
    f1[...] = total_of(v1, 8)
    for j in range(15):
        to = place(j, z * 2 + 1 - core, 16)
        send(11, f1, rows_of(out_ref, 256 + zc * 16, 16), (y * NZC + (to // 2) * 2 + 1 - to % 2, feat))
    own1 = pltpu.make_async_copy(f1, rows_of(out_ref, 256 + zc * 16, 16), load_sem.at[10])
    own1.start()
    own0.wait()
    own1.wait()
    arrive(10, out_ref, 240)
    arrive(11, out_ref, 240)

    for copies in sent:
        copies.wait_send()


def widen(sums, first_ref, second_ref):
    for h in range(2):
        first_ref[:, h * 128 : (h + 1) * 128] = sums[h * 256 : h * 256 + 192].astype(F32)
        second_ref[:, h * 128 : (h + 1) * 128] = sums[h * 256 + 192 : h * 256 + 256].astype(F32)


def body(
    features, pre_act, out_grad, w_second, adj_tiles, tile_cols, tile_live, halo_counts, border_rows
):
    anywhere = pl.BlockSpec(memory_space=pl.ANY)
    vmem = pl.BlockSpec(memory_space=pltpu.VMEM)
    half = pltpu.VMEM((256, 128), BF16)
    square = pltpu.VMEM((256, 256), BF16)
    grads = pl.pallas_call(
        kernel,
        out_shape=pltpu.VMEM((512, 128), BF16),
        in_specs=[anywhere] * 9,
        out_specs=anywhere,
        scratch_shapes=[
            pltpu.VMEM((192, 256), BF16),
            square,
            pltpu.VMEM((64, 256), BF16),
            pltpu.VMEM((64, 256), BF16),
            pltpu.VMEM((2, 6, 128, 128), jnp.int32),
            pltpu.VMEM((1, 128), jnp.int32),
            pltpu.VMEM((2, 128), jnp.int32),
            pltpu.SMEM((2, 6), jnp.int32),
            pltpu.SMEM((2,), jnp.int32),
            pltpu.VMEM((256, 512), BF16),
            square, square, square, square, half, half,
            square, square, square,
            pltpu.VMEM((128, 128), BF16),
            pltpu.VMEM((512, 128), BF16),
            half, half, half, half,
            pltpu.VMEM((16, 128), BF16),
            pltpu.VMEM((16, 128), BF16),
            pltpu.VMEM((128, 128), BF16),
            pltpu.VMEM((128, 128), BF16),
            pltpu.VMEM((16, 128), BF16),
            pltpu.VMEM((16, 128), BF16),
            pltpu.SemaphoreType.DMA((11,)),
            pltpu.SemaphoreType.DMA((PHASES,)),
            pltpu.SemaphoreType.DMA((PHASES,)),
            pltpu.SemaphoreType.REGULAR,
        ],
        compiler_params=pltpu.CompilerParams(collective_id=0, has_side_effects=True, vmem_limit_bytes=60 * 1024 * 1024),
        name="sage_backward",
    )(
        features.T, pre_act, out_grad.T, w_second.T, adj_tiles, tile_cols, tile_live,
        halo_counts.reshape(1, 128), border_rows.T,
    )
    grad_first, grad_second_t = pl.pallas_call(
        widen,
        out_shape=(
            jax.ShapeDtypeStruct((192, 256), F32),
            jax.ShapeDtypeStruct((64, 256), F32),
        ),
        in_specs=[vmem],
        out_specs=(vmem, vmem),
        compiler_params=pltpu.CompilerParams(vmem_limit_bytes=4 * 1024 * 1024),
        name="widen",
    )(grads)
    return grad_first, grad_second_t.T


def solution(mesh):
    in_specs = (
        P("dom", "feat"),
        P("dom", None),
        P("dom", "feat"),
        P(None, "feat"),
        P("dom", None, None, None),
        P("dom", None),
        P("dom"),
        P("dom"),
        P("dom", None),
    )
    out_specs = (P("feat", None), P(None, "feat"))
    return jax.shard_map(body, mesh=mesh, in_specs=in_specs, out_specs=out_specs, check_vma=False)
```

```python
import jax
import jax.numpy as jnp
from jax import lax
from jax.experimental import pallas as pl
from jax.experimental.pallas import tpu as pltpu
from jax.sharding import PartitionSpec as P

MESH = pl.DeviceIdType.MESH
BF16 = jnp.bfloat16
F32 = jnp.float32

NY = 8
NZC = 16
NZ = 8
NX = 4
PHASES = 12
FAR_8 = (4, 3, 5, 2, 6, 1, 7)
FAR_16 = (8, 7, 9, 6, 10, 5, 11, 4, 12, 3, 13, 2, 14, 1, 15)
FAR_4 = (2, 1, 3)


def dot(a, b):
    return lax.dot_general(a, b, (((1,), (0,)), ((), ())), preferred_element_type=F32)


def dot_nt(a, b):
    return lax.dot_general(a, b, (((1,), (1,)), ((), ())), preferred_element_type=F32)


def rows_of(ref, start, size):
    return ref.at[pl.ds(pl.multiple_of(start, size), size)]


def kernel(
    ft_hbm, pa_hbm, gt_hbm, wt_hbm, adj_hbm, cols_hbm, live_hbm, hc_hbm, br_hbm,
    out_ref,
    ft, pa, gt, wt, adj, hc, br, cols_ref, live_ref,
    amat, s0, r0, t0, u0, s1, r1, wall, sall, oall, t1s, su,
    q0s, q1s, q0, q1, w0, w1, v0, v1, f0, f1,
    load_sem, send_sem, recv_sem, ready_sem,
):
    dom = lax.axis_index("dom")
    feat = lax.axis_index("feat")
    y = dom // NZC
    zc = dom % NZC
    z = zc // 2
    core = dom % 2
    yc = y * 2 + core

    def dom_y(k):
        return ((y + k) % NY) * NZC + zc

    def dom_zc(k):
        return y * NZC + (zc + k) % NZC

    def place(j, own, size):
        return j + (j + size - own) // size

    barrier = pltpu.get_barrier_semaphore()

    def greet(d, f):
        pl.semaphore_signal(barrier, inc=1, device_id=(d, f), device_id_type=MESH)

    for k in FAR_16:
        greet(dom_zc(k), feat)
    for k in FAR_8:
        greet(dom_y(k), feat)
        greet(((y + k) % NY) * NZC + z * 2 + (1 - core), feat)
    for k in FAR_4:
        greet(dom, (feat + k) % NX)
    loads = []
    for i, (src, dst) in enumerate(
        [(br_hbm, br), (adj_hbm, adj), (ft_hbm, ft), (hc_hbm, hc), (gt_hbm, gt), (wt_hbm, wt), (pa_hbm, pa), (cols_hbm, cols_ref), (live_hbm, live_ref)]
    ):
        copy = pltpu.make_async_copy(src, dst, load_sem.at[i])
        copy.start()
        loads.append(copy)
    ld_br, ld_adj, ld_ft, ld_hc, ld_gt, ld_wt, ld_pa, ld_cols, ld_live = loads

    partners = (NY - 1) * 2 + (NZC - 1) + (NX - 1)

    def send(phase, src, dst, device):
        copy = pltpu.make_async_remote_copy(
            src_ref=src,
            dst_ref=dst,
            send_sem=send_sem.at[phase],
            recv_sem=recv_sem.at[phase],
            device_id=device,
            device_id_type=MESH,
        )
        copy.start()

    def scatter_y(phase, src, dst, rows):
        for k in FAR_8:
            send(phase, rows_of(src, ((y + k) % NY) * rows, rows), rows_of(dst, y * rows, rows), (dom_y(k), feat))
        rows_of(dst, y * rows, rows)[...] = rows_of(src, y * rows, rows)[...]

    def scatter_zc(phase, src, dst, rows):
        for k in FAR_16:
            send(phase, rows_of(src, ((zc + k) % NZC) * rows, rows), rows_of(dst, zc * rows, rows), (dom_zc(k), feat))
        rows_of(dst, zc * rows, rows)[...] = rows_of(src, zc * rows, rows)[...]

    def all_of(phase, ref, rows):
        return pltpu.make_async_remote_copy(
            src_ref=ref.at[pl.ds(0, rows)],
            dst_ref=ref.at[pl.ds(0, rows)],
            send_sem=send_sem.at[phase],
            recv_sem=recv_sem.at[phase],
            device_id=(dom_y(1), feat),
            device_id_type=MESH,
        )

    sent = []

    def arrive(phase, ref, rows):
        copies = all_of(phase, ref, rows)
        copies.wait_recv()
        sent.append(copies)

    n = 256
    rows_i = lax.broadcasted_iota(jnp.int32, (n, n), 0)
    lanes_i = lax.broadcasted_iota(jnp.int32, (n, n), 1)
    one_hot = lambda cond: jnp.where(cond, 1.0, 0.0).astype(BF16)
    eye = one_hot(rows_i == lanes_i)
    perm = one_hot(lanes_i == ((rows_i >> 1) & 7) * 32 + (rows_i >> 4) * 2 + (rows_i & 1))
    perm_p = one_hot(lanes_i == (rows_i & 15) * 16 + ((rows_i >> 4) & 7) * 2 + (rows_i >> 7))
    by_c = one_hot(lanes_i == (rows_i & 127) * 2 + (rows_i >> 7))
    eye128 = one_hot(
        lax.broadcasted_iota(jnp.int32, (128, 128), 0) == lax.broadcasted_iota(jnp.int32, (128, 128), 1)
    )
    peer_i = lax.broadcasted_iota(jnp.int32, (128, n), 0)
    slot_i = lax.broadcasted_iota(jnp.int32, (128, n), 1)
    even = one_hot(slot_i == 2 * peer_i)
    odd = one_hot(slot_i == 2 * peer_i + 1)

    ld_br.wait()
    border = br[...].astype(F32).astype(BF16)
    slot_row = dot(jnp.broadcast_to(border[0:1], (16, 128)), even) + dot(
        jnp.broadcast_to(border[1:2], (16, 128)), odd
    )
    hot_t = one_hot(rows_i.astype(F32) == slot_row[0:1])
    hot = dot_nt(eye, hot_t).astype(BF16)
    hot_c = dot_nt(by_c, hot_t).astype(BF16)

    ld_hc.wait()
    counts = jnp.broadcast_to(hc[...].astype(F32).astype(BF16), (16, 128))
    slot_counts = dot(counts, even + odd)[0:1]
    parity = (lax.broadcasted_iota(jnp.int32, (1, n), 1) & 1).astype(F32)
    flags = jnp.where(parity < slot_counts, 1.0, 0.0)
    ld_cols.wait()
    ld_live.wait()
    ld_adj.wait()
    for b in range(2):
        for cb in range(4):
            total = jnp.zeros((128, 128), jnp.int32)
            for s in range(6):
                keep = jnp.logical_and(cols_ref[b, s] == cb, s < live_ref[b])
                total = total + (adj[b, s] & jnp.where(keep, -1, 0))
            total = total.astype(F32)
            if cb >= 2:
                total = total * flags[:, (cb - 2) * 128 : (cb - 1) * 128]
            amat[b * 128 : (b + 1) * 128, cb * 128 : (cb + 1) * 128] = total.astype(BF16)
    inverse = 1.0 / dot_nt(jnp.ones((16, 512), BF16), amat[...])[0:1]

    ld_gt.wait()
    scaled = gt[...].astype(F32) * inverse
    high = scaled.astype(BF16)
    low = (scaled - high.astype(F32)).astype(BF16)
    spread = dot(jnp.concatenate([high, low], axis=0), amat[...])
    spread = spread[0:64] + spread[64:128]
    own_part = spread[:, 0:256]
    halo_part = spread[:, 256:512].astype(BF16)
    s1[...] = dot_nt(perm, jnp.concatenate([halo_part, halo_part], axis=0)).astype(BF16)

    pl.semaphore_wait(barrier, partners)
    for k in FAR_8:
        pl.semaphore_signal(ready_sem, inc=1, device_id=(dom_y(k), feat), device_id_type=MESH)
    scatter_zc(2, s1, r1, 16)
    ld_ft.wait()
    s0[...] = dot_nt(hot, jnp.concatenate([ft[...], jnp.zeros((64, n), BF16)], axis=0)).astype(BF16)
    scatter_y(0, s0, r0, 32)
    ld_wt.wait()
    for k in FAR_4:
        send(4, wt, rows_of(wall, feat * 64, 64), (dom, (feat + k) % NX))
    rows_of(wall, feat * 64, 64)[...] = wt[...]

    rows_of(oall, feat * 64, 64)[...] = own_part.astype(BF16)
    for k in FAR_4:
        send(5, rows_of(oall, feat * 64, 64), rows_of(oall, feat * 64, 64), (dom, (feat + k) % NX))

    a_own = amat[:, 0:256]
    a_halo = amat[:, 256:512]
    a_halo_p = dot_nt(a_halo, perm).astype(BF16)
    mixed = dot_nt(ft[...], a_own)
    ld_pa.wait()
    pre = pa[...].astype(F32)
    act = jnp.maximum(pre, 0.0).astype(BF16)
    mask_t = dot_nt(eye, one_hot(pre > 0.0))

    arrive(2, r1, 240)
    pl.semaphore_wait(ready_sem, NY - 1)
    packed = dot(perm_p, r1[...])
    t1s[...] = jnp.where(
        lax.broadcasted_iota(jnp.int32, (128, 128), 1) < 64, packed[0:128], packed[128:256]
    ).astype(BF16)
    for k in FAR_8 + (0,):
        for m in FAR_4 + (0,):
            if k + m > 0:
                send(
                    3,
                    rows_of(t1s, ((y + k) % NY) * 16, 16),
                    rows_of(su, feat * 128 + y * 16, 16),
                    (dom_y(k), (feat + m) % NX),
                )
    rows_of(su, feat * 128 + y * 16, 16)[...] = rows_of(t1s, y * 16, 16)[...]
    arrive(0, r0, 224)
    t0[...] = dot(perm, r0[...]).astype(BF16)
    scatter_zc(1, t0, u0, 16)

    arrive(5, oall, 192)
    own_all = oall[...].astype(F32)
    arrive(4, wall, 192)
    w_full = dot_nt(eye, wall[...]).astype(BF16)

    arrive(3, su, 496)
    x_s = dot_nt(eye128, su[...]).astype(BF16)
    even_part = jnp.concatenate([x_s[0:64, i * 128 : (i + 1) * 128] for i in range(NX)], axis=0)
    odd_part = jnp.concatenate([x_s[64:128, i * 128 : (i + 1) * 128] for i in range(NX)], axis=0)
    gathered = own_all + dot(jnp.concatenate([even_part, odd_part], axis=1), hot_c)
    sall[...] = gathered.astype(BF16)

    arrive(1, u0, 240)
    x0 = dot_nt(eye, u0[...]).astype(BF16)
    mixed_in = ((mixed + dot_nt(x0[0:192], a_halo_p)) * inverse).astype(BF16)

    second = dot(rows_of(sall, feat * 64, 64)[...], act)
    q0s[192:256] = second[:, 0:128].astype(BF16)
    q1s[192:256] = second[:, 128:256].astype(BF16)
    grad_act = dot(w_full, sall[...])
    grad_pre = jnp.where(mask_t > 0.5, grad_act, 0.0).astype(BF16)
    first = dot_nt(mixed_in, grad_pre)
    q0s[0:192] = first[:, 0:128].astype(BF16)
    q1s[0:192] = first[:, 128:256].astype(BF16)

    on_y = lambda k: (((y + k) % NY) * NZC + z * 2 + 1, feat)
    on_z = lambda k: (y * NZC + ((z + k) % NZ) * 2 + 1, feat)

    def scatter_to_owner(k):
        send(6, rows_of(q0s, ((y + k) % NY) * 32, 32), rows_of(q0, yc * 32, 32), on_y(k))
        send(7, rows_of(q1s, ((z + k) % NZ) * 32, 32), rows_of(q1, zc * 32, 32), on_z(k))

    for k in FAR_8:
        scatter_to_owner(k)

    def total_of(ref, members):
        total = ref[0:32].astype(F32)
        for i in range(1, members):
            total = total + ref[i * 32 : (i + 1) * 32].astype(F32)
        return total.astype(BF16)

    @pl.when(core == 0)
    def _():
        scatter_to_owner(0)
        all_of(10, out_ref, 256).wait_recv()
        all_of(11, out_ref, 256).wait_recv()
        all_of(6, q0, 256).wait_send()
        all_of(7, q1, 256).wait_send()

    @pl.when(core == 1)
    def _():
        rows_of(q0, yc * 32, 32)[...] = rows_of(q0s, y * 32, 32)[...]
        rows_of(q1, zc * 32, 32)[...] = rows_of(q1s, z * 32, 32)[...]
        all_of(6, q0, 480).wait_recv()
        part0 = total_of(q0, 16)
        w0[...] = part0
        for j in range(NZ - 1):
            send(8, w0, rows_of(v0, z * 32, 32), (y * NZC + place(j, z, NZ) * 2 + 1, feat))
        rows_of(v0, z * 32, 32)[...] = part0
        all_of(7, q1, 480).wait_recv()
        part1 = total_of(q1, 16)
        w1[...] = part1
        for j in range(NY - 1):
            send(9, w1, rows_of(v1, y * 32, 32), (place(j, y, NY) * NZC + zc, feat))
        rows_of(v1, y * 32, 32)[...] = part1

        all_of(8, v0, 224).wait_recv()
        f0[...] = total_of(v0, 8)
        for j in range(15):
            to = place(j, y * 2, 16)
            send(10, f0, rows_of(out_ref, y * 32, 32), ((to // 2) * NZC + z * 2 + 1 - to % 2, feat))
        own0 = pltpu.make_async_copy(f0, rows_of(out_ref, y * 32, 32), load_sem.at[9])
        own0.start()
        all_of(9, v1, 224).wait_recv()
        f1[...] = total_of(v1, 8)
        for j in range(15):
            to = place(j, z * 2, 16)
            send(11, f1, rows_of(out_ref, 256 + z * 32, 32), (y * NZC + (to // 2) * 2 + 1 - to % 2, feat))
        own1 = pltpu.make_async_copy(f1, rows_of(out_ref, 256 + z * 32, 32), load_sem.at[10])
        own1.start()
        own0.wait()
        own1.wait()
        all_of(10, out_ref, 224).wait_recv()
        all_of(11, out_ref, 224).wait_recv()
        all_of(6, q0, 224).wait_send()
        all_of(7, q1, 224).wait_send()
        all_of(8, v0, 224).wait_send()
        all_of(9, v1, 224).wait_send()
        all_of(10, q0, 480).wait_send()
        all_of(11, q1, 480).wait_send()

    for copies in sent:
        copies.wait_send()


def widen(sums, first_ref, second_ref):
    for h in range(2):
        first_ref[:, h * 128 : (h + 1) * 128] = sums[h * 256 : h * 256 + 192].astype(F32)
        second_ref[:, h * 128 : (h + 1) * 128] = sums[h * 256 + 192 : h * 256 + 256].astype(F32)


def body(
    features, pre_act, out_grad, w_second, adj_tiles, tile_cols, tile_live, halo_counts, border_rows
):
    anywhere = pl.BlockSpec(memory_space=pl.ANY)
    vmem = pl.BlockSpec(memory_space=pltpu.VMEM)
    half = pltpu.VMEM((256, 128), BF16)
    square = pltpu.VMEM((256, 256), BF16)
    grads = pl.pallas_call(
        kernel,
        out_shape=pltpu.VMEM((512, 128), BF16),
        in_specs=[anywhere] * 9,
        out_specs=anywhere,
        scratch_shapes=[
            pltpu.VMEM((192, 256), BF16),
            square,
            pltpu.VMEM((64, 256), BF16),
            pltpu.VMEM((64, 256), BF16),
            pltpu.VMEM((2, 6, 128, 128), jnp.int32),
            pltpu.VMEM((1, 128), jnp.int32),
            pltpu.VMEM((2, 128), jnp.int32),
            pltpu.SMEM((2, 6), jnp.int32),
            pltpu.SMEM((2,), jnp.int32),
            pltpu.VMEM((256, 512), BF16),
            square, square, square, square, half, half,
            square, square, square,
            pltpu.VMEM((128, 128), BF16),
            pltpu.VMEM((512, 128), BF16),
            half, half,
            pltpu.VMEM((512, 128), BF16),
            pltpu.VMEM((512, 128), BF16),
            pltpu.VMEM((32, 128), BF16), pltpu.VMEM((32, 128), BF16), half, half, pltpu.VMEM((32, 128), BF16), pltpu.VMEM((32, 128), BF16),
            pltpu.SemaphoreType.DMA((11,)),
            pltpu.SemaphoreType.DMA((PHASES,)),
            pltpu.SemaphoreType.DMA((PHASES,)),
            pltpu.SemaphoreType.REGULAR,
        ],
        compiler_params=pltpu.CompilerParams(collective_id=0, has_side_effects=True, vmem_limit_bytes=60 * 1024 * 1024),
        name="sage_backward",
    )(
        features.T, pre_act, out_grad.T, w_second.T, adj_tiles, tile_cols, tile_live,
        halo_counts.reshape(1, 128), border_rows.T,
    )
    grad_first, grad_second_t = pl.pallas_call(
        widen,
        out_shape=(
            jax.ShapeDtypeStruct((192, 256), F32),
            jax.ShapeDtypeStruct((64, 256), F32),
        ),
        in_specs=[vmem],
        out_specs=(vmem, vmem),
        compiler_params=pltpu.CompilerParams(vmem_limit_bytes=4 * 1024 * 1024),
        name="widen",
    )(grads)
    return grad_first, grad_second_t.T


def solution(mesh):
    in_specs = (
        P("dom", "feat"),
        P("dom", None),
        P("dom", "feat"),
        P(None, "feat"),
        P("dom", None, None, None),
        P("dom", None),
        P("dom"),
        P("dom"),
        P("dom", None),
    )
    out_specs = (P("feat", None), P(None, "feat"))
    return jax.shard_map(body, mesh=mesh, in_specs=in_specs, out_specs=out_specs, check_vma=False)
```

```python
import jax
import jax.numpy as jnp
from jax import lax
from jax.experimental import pallas as pl
from jax.experimental.pallas import tpu as pltpu
from jax.sharding import PartitionSpec as P

MESH = pl.DeviceIdType.MESH
BF16 = jnp.bfloat16
F32 = jnp.float32

NY = 8
NZC = 16
NZ = 8
NX = 4
PHASES = 12
FAR_8 = (4, 3, 5, 2, 6, 1, 7)
FAR_16 = (8, 7, 9, 6, 10, 5, 11, 4, 12, 3, 13, 2, 14, 1, 15)
FAR_4 = (2, 1, 3)


def dot(a, b):
    return lax.dot_general(a, b, (((1,), (0,)), ((), ())), preferred_element_type=F32)


def dot_nt(a, b):
    return lax.dot_general(a, b, (((1,), (1,)), ((), ())), preferred_element_type=F32)


def rows_of(ref, start, size):
    return ref.at[pl.ds(pl.multiple_of(start, size), size)]


def kernel(
    ft_hbm, pa_hbm, gt_hbm, wt_hbm, adj_hbm, cols_hbm, live_hbm, hc_hbm, br_hbm,
    out_ref,
    ft, pa, gt, wt, adj, hc, br, cols_ref, live_ref,
    amat, s0, r0, t0, u0, s1, r1, wall, sall, oall, t1s, su,
    q0s, q1s, q0, q1, w0, w1, v0, v1, f0, f1,
    load_sem, send_sem, recv_sem, ready_sem,
):
    dom = lax.axis_index("dom")
    feat = lax.axis_index("feat")
    y = dom // NZC
    zc = dom % NZC
    z = zc // 2
    core = dom % 2
    yc = y * 2 + core

    def dom_y(k):
        return ((y + k) % NY) * NZC + zc

    def dom_zc(k):
        return y * NZC + (zc + k) % NZC

    def place(j, own, size):
        return j + (j + size - own) // size

    barrier = pltpu.get_barrier_semaphore()

    def greet(d, f):
        pl.semaphore_signal(barrier, inc=1, device_id=(d, f), device_id_type=MESH)

    for k in FAR_16:
        greet(dom_zc(k), feat)
    for k in FAR_8:
        greet(dom_y(k), feat)
        greet(((y + k) % NY) * NZC + z * 2 + (1 - core), feat)
    for k in FAR_4:
        greet(dom, (feat + k) % NX)
    loads = []
    for i, (src, dst) in enumerate(
        [(br_hbm, br), (adj_hbm, adj), (ft_hbm, ft), (hc_hbm, hc), (gt_hbm, gt), (wt_hbm, wt), (pa_hbm, pa), (cols_hbm, cols_ref), (live_hbm, live_ref)]
    ):
        copy = pltpu.make_async_copy(src, dst, load_sem.at[i])
        copy.start()
        loads.append(copy)
    ld_br, ld_adj, ld_ft, ld_hc, ld_gt, ld_wt, ld_pa, ld_cols, ld_live = loads

    partners = (NY - 1) * 2 + (NZC - 1) + (NX - 1)

    def send(phase, src, dst, device):
        copy = pltpu.make_async_remote_copy(
            src_ref=src,
            dst_ref=dst,
            send_sem=send_sem.at[phase],
            recv_sem=recv_sem.at[phase],
            device_id=device,
            device_id_type=MESH,
        )
        copy.start()

    def scatter_y(phase, src, dst, rows):
        for k in FAR_8:
            send(phase, rows_of(src, ((y + k) % NY) * rows, rows), rows_of(dst, y * rows, rows), (dom_y(k), feat))
        rows_of(dst, y * rows, rows)[...] = rows_of(src, y * rows, rows)[...]

    def scatter_zc(phase, src, dst, rows):
        for k in FAR_16:
            send(phase, rows_of(src, ((zc + k) % NZC) * rows, rows), rows_of(dst, zc * rows, rows), (dom_zc(k), feat))
        rows_of(dst, zc * rows, rows)[...] = rows_of(src, zc * rows, rows)[...]

    def all_of(phase, ref, rows):
        return pltpu.make_async_remote_copy(
            src_ref=ref.at[pl.ds(0, rows)],
            dst_ref=ref.at[pl.ds(0, rows)],
            send_sem=send_sem.at[phase],
            recv_sem=recv_sem.at[phase],
            device_id=(dom_y(1), feat),
            device_id_type=MESH,
        )

    sent = []

    def arrive(phase, ref, rows):
        copies = all_of(phase, ref, rows)
        copies.wait_recv()
        sent.append(copies)

    n = 256
    rows_i = lax.broadcasted_iota(jnp.int32, (n, n), 0)
    lanes_i = lax.broadcasted_iota(jnp.int32, (n, n), 1)
    one_hot = lambda cond: jnp.where(cond, 1.0, 0.0).astype(BF16)
    eye = one_hot(rows_i == lanes_i)
    perm = one_hot(lanes_i == ((rows_i >> 1) & 7) * 32 + (rows_i >> 4) * 2 + (rows_i & 1))
    perm_p = one_hot(lanes_i == (rows_i & 15) * 16 + ((rows_i >> 4) & 7) * 2 + (rows_i >> 7))
    by_c = one_hot(lanes_i == (rows_i & 127) * 2 + (rows_i >> 7))
    eye128 = one_hot(
        lax.broadcasted_iota(jnp.int32, (128, 128), 0) == lax.broadcasted_iota(jnp.int32, (128, 128), 1)
    )
    peer_i = lax.broadcasted_iota(jnp.int32, (128, n), 0)
    slot_i = lax.broadcasted_iota(jnp.int32, (128, n), 1)
    even = one_hot(slot_i == 2 * peer_i)
    odd = one_hot(slot_i == 2 * peer_i + 1)

    ld_br.wait()
    border = br[...].astype(F32).astype(BF16)
    slot_row = dot(jnp.broadcast_to(border[0:1], (16, 128)), even) + dot(
        jnp.broadcast_to(border[1:2], (16, 128)), odd
    )
    hot_t = one_hot(rows_i.astype(F32) == slot_row[0:1])
    hot = dot_nt(eye, hot_t).astype(BF16)
    hot_c = dot_nt(by_c, hot_t).astype(BF16)

    ld_ft.wait()
    s0[...] = dot_nt(hot, jnp.concatenate([ft[...], jnp.zeros((64, n), BF16)], axis=0)).astype(BF16)

    ld_hc.wait()
    counts = jnp.broadcast_to(hc[...].astype(F32).astype(BF16), (16, 128))
    slot_counts = dot(counts, even + odd)[0:1]
    parity = (lax.broadcasted_iota(jnp.int32, (1, n), 1) & 1).astype(F32)
    flags = jnp.where(parity < slot_counts, 1.0, 0.0)
    ld_cols.wait()
    ld_live.wait()
    ld_adj.wait()
    for b in range(2):
        for cb in range(4):
            total = jnp.zeros((128, 128), jnp.int32)
            for s in range(6):
                keep = jnp.logical_and(cols_ref[b, s] == cb, s < live_ref[b])
                total = total + (adj[b, s] & jnp.where(keep, -1, 0))
            total = total.astype(F32)
            if cb >= 2:
                total = total * flags[:, (cb - 2) * 128 : (cb - 1) * 128]
            amat[b * 128 : (b + 1) * 128, cb * 128 : (cb + 1) * 128] = total.astype(BF16)
    inverse = 1.0 / dot_nt(jnp.ones((16, 512), BF16), amat[...])[0:1]

    ld_gt.wait()
    scaled = gt[...].astype(F32) * inverse
    high = scaled.astype(BF16)
    low = (scaled - high.astype(F32)).astype(BF16)
    spread = dot(jnp.concatenate([high, low], axis=0), amat[...])
    spread = spread[0:64] + spread[64:128]
    own_part = spread[:, 0:256]
    halo_part = spread[:, 256:512].astype(BF16)
    s1[...] = dot_nt(perm, jnp.concatenate([halo_part, halo_part], axis=0)).astype(BF16)

    pl.semaphore_wait(barrier, partners)
    for k in FAR_8:
        pl.semaphore_signal(ready_sem, inc=1, device_id=(dom_y(k), feat), device_id_type=MESH)
    scatter_zc(2, s1, r1, 16)
    scatter_y(0, s0, r0, 32)
    ld_wt.wait()
    for k in FAR_4:
        send(4, wt, rows_of(wall, feat * 64, 64), (dom, (feat + k) % NX))
    rows_of(wall, feat * 64, 64)[...] = wt[...]

    rows_of(oall, feat * 64, 64)[...] = own_part.astype(BF16)
    for k in FAR_4:
        send(5, rows_of(oall, feat * 64, 64), rows_of(oall, feat * 64, 64), (dom, (feat + k) % NX))

    a_own = amat[:, 0:256]
    a_halo = amat[:, 256:512]
    a_halo_p = dot_nt(a_halo, perm).astype(BF16)
    mixed = dot_nt(ft[...], a_own)
    ld_pa.wait()
    pre = pa[...].astype(F32)
    act = jnp.maximum(pre, 0.0).astype(BF16)
    mask_t = dot_nt(eye, one_hot(pre > 0.0))

    arrive(2, r1, 240)
    pl.semaphore_wait(ready_sem, NY - 1)
    packed = dot(perm_p, r1[...])
    t1s[...] = jnp.where(
        lax.broadcasted_iota(jnp.int32, (128, 128), 1) < 64, packed[0:128], packed[128:256]
    ).astype(BF16)
    for k in FAR_8 + (0,):
        for m in FAR_4 + (0,):
            if k + m > 0:
                send(
                    3,
                    rows_of(t1s, ((y + k) % NY) * 16, 16),
                    rows_of(su, feat * 128 + y * 16, 16),
                    (dom_y(k), (feat + m) % NX),
                )
    rows_of(su, feat * 128 + y * 16, 16)[...] = rows_of(t1s, y * 16, 16)[...]
    arrive(0, r0, 224)
    t0[...] = dot(perm, r0[...]).astype(BF16)
    scatter_zc(1, t0, u0, 16)

    arrive(5, oall, 192)
    own_all = oall[...].astype(F32)
    arrive(4, wall, 192)
    w_full = dot_nt(eye, wall[...]).astype(BF16)

    arrive(3, su, 496)
    x_s = dot_nt(eye128, su[...]).astype(BF16)
    even_part = jnp.concatenate([x_s[0:64, i * 128 : (i + 1) * 128] for i in range(NX)], axis=0)
    odd_part = jnp.concatenate([x_s[64:128, i * 128 : (i + 1) * 128] for i in range(NX)], axis=0)
    gathered = own_all + dot(jnp.concatenate([even_part, odd_part], axis=1), hot_c)
    sall[...] = gathered.astype(BF16)

    arrive(1, u0, 240)
    x0 = dot_nt(eye, u0[...]).astype(BF16)
    mixed_in = ((mixed + dot_nt(x0[0:192], a_halo_p)) * inverse).astype(BF16)

    second = dot(rows_of(sall, feat * 64, 64)[...], act)
    q0s[192:256] = second[:, 0:128].astype(BF16)
    q1s[192:256] = second[:, 128:256].astype(BF16)
    grad_act = dot(w_full, sall[...])
    grad_pre = jnp.where(mask_t > 0.5, grad_act, 0.0).astype(BF16)
    first = dot_nt(mixed_in, grad_pre)
    q0s[0:192] = first[:, 0:128].astype(BF16)
    q1s[0:192] = first[:, 128:256].astype(BF16)

    on_y = lambda k: (((y + k) % NY) * NZC + z * 2 + 1, feat)
    on_z = lambda k: (y * NZC + ((z + k) % NZ) * 2 + 1, feat)

    def scatter_to_owner(k):
        send(6, rows_of(q0s, ((y + k) % NY) * 32, 32), rows_of(q0, yc * 32, 32), on_y(k))
        send(7, rows_of(q1s, ((z + k) % NZ) * 32, 32), rows_of(q1, zc * 32, 32), on_z(k))

    for k in FAR_8:
        scatter_to_owner(k)

    def total_of(ref, members):
        total = ref[0:32].astype(F32)
        for i in range(1, members):
            total = total + ref[i * 32 : (i + 1) * 32].astype(F32)
        return total.astype(BF16)

    @pl.when(core == 0)
    def _():
        scatter_to_owner(0)
        all_of(10, out_ref, 256).wait_recv()
        all_of(11, out_ref, 256).wait_recv()
        all_of(6, q0, 256).wait_send()
        all_of(7, q1, 256).wait_send()

    @pl.when(core == 1)
    def _():
        rows_of(q0, yc * 32, 32)[...] = rows_of(q0s, y * 32, 32)[...]
        rows_of(q1, zc * 32, 32)[...] = rows_of(q1s, z * 32, 32)[...]
        all_of(6, q0, 480).wait_recv()
        part0 = total_of(q0, 16)
        w0[...] = part0
        for k in FAR_8:
            send(8, w0, rows_of(v0, z * 32, 32), on_z(k))
        rows_of(v0, z * 32, 32)[...] = part0
        all_of(7, q1, 480).wait_recv()
        part1 = total_of(q1, 16)
        w1[...] = part1
        for k in FAR_8:
            send(9, w1, rows_of(v1, y * 32, 32), (dom_y(k), feat))
        rows_of(v1, y * 32, 32)[...] = part1

        all_of(8, v0, 224).wait_recv()
        f0[...] = total_of(v0, 8)
        for k in FAR_8:
            send(10, f0, rows_of(out_ref, y * 32, 32), (dom_y(k), feat))
        for k in FAR_8 + (0,):
            send(10, f0, rows_of(out_ref, y * 32, 32), (dom_y(k) - 1, feat))
        own0 = pltpu.make_async_copy(f0, rows_of(out_ref, y * 32, 32), load_sem.at[9])
        own0.start()
        all_of(9, v1, 224).wait_recv()
        f1[...] = total_of(v1, 8)
        for k in FAR_8:
            send(11, f1, rows_of(out_ref, 256 + z * 32, 32), on_z(k))
        for k in FAR_8 + (0,):
            send(11, f1, rows_of(out_ref, 256 + z * 32, 32), (on_z(k)[0] - 1, feat))
        own1 = pltpu.make_async_copy(f1, rows_of(out_ref, 256 + z * 32, 32), load_sem.at[10])
        own1.start()
        own0.wait()
        own1.wait()
        all_of(10, out_ref, 224).wait_recv()
        all_of(11, out_ref, 224).wait_recv()
        all_of(6, q0, 224).wait_send()
        all_of(7, q1, 224).wait_send()
        all_of(8, v0, 224).wait_send()
        all_of(9, v1, 224).wait_send()
        all_of(10, q0, 480).wait_send()
        all_of(11, q1, 480).wait_send()

    for copies in sent:
        copies.wait_send()


def widen(sums, first_ref, second_ref):
    for h in range(2):
        first_ref[:, h * 128 : (h + 1) * 128] = sums[h * 256 : h * 256 + 192].astype(F32)
        second_ref[:, h * 128 : (h + 1) * 128] = sums[h * 256 + 192 : h * 256 + 256].astype(F32)


def body(
    features, pre_act, out_grad, w_second, adj_tiles, tile_cols, tile_live, halo_counts, border_rows
):
    anywhere = pl.BlockSpec(memory_space=pl.ANY)
    vmem = pl.BlockSpec(memory_space=pltpu.VMEM)
    half = pltpu.VMEM((256, 128), BF16)
    square = pltpu.VMEM((256, 256), BF16)
    grads = pl.pallas_call(
        kernel,
        out_shape=pltpu.VMEM((512, 128), BF16),
        in_specs=[anywhere] * 9,
        out_specs=anywhere,
        scratch_shapes=[
            pltpu.VMEM((192, 256), BF16),
            square,
            pltpu.VMEM((64, 256), BF16),
            pltpu.VMEM((64, 256), BF16),
            pltpu.VMEM((2, 6, 128, 128), jnp.int32),
            pltpu.VMEM((1, 128), jnp.int32),
            pltpu.VMEM((2, 128), jnp.int32),
            pltpu.SMEM((2, 6), jnp.int32),
            pltpu.SMEM((2,), jnp.int32),
            pltpu.VMEM((256, 512), BF16),
            square, square, square, square, half, half,
            square, square, square,
            pltpu.VMEM((128, 128), BF16),
            pltpu.VMEM((512, 128), BF16),
            half, half,
            pltpu.VMEM((512, 128), BF16),
            pltpu.VMEM((512, 128), BF16),
            pltpu.VMEM((32, 128), BF16), pltpu.VMEM((32, 128), BF16), half, half, pltpu.VMEM((32, 128), BF16), pltpu.VMEM((32, 128), BF16),
            pltpu.SemaphoreType.DMA((11,)),
            pltpu.SemaphoreType.DMA((PHASES,)),
            pltpu.SemaphoreType.DMA((PHASES,)),
            pltpu.SemaphoreType.REGULAR,
        ],
        compiler_params=pltpu.CompilerParams(collective_id=0, has_side_effects=True, vmem_limit_bytes=60 * 1024 * 1024),
        name="sage_backward",
    )(
        features.T, pre_act, out_grad.T, w_second.T, adj_tiles, tile_cols, tile_live,
        halo_counts.reshape(1, 128), border_rows.T,
    )
    grad_first, grad_second_t = pl.pallas_call(
        widen,
        out_shape=(
            jax.ShapeDtypeStruct((192, 256), F32),
            jax.ShapeDtypeStruct((64, 256), F32),
        ),
        in_specs=[vmem],
        out_specs=(vmem, vmem),
        compiler_params=pltpu.CompilerParams(vmem_limit_bytes=4 * 1024 * 1024),
        name="widen",
    )(grads)
    return grad_first, grad_second_t.T


def solution(mesh):
    in_specs = (
        P("dom", "feat"),
        P("dom", None),
        P("dom", "feat"),
        P(None, "feat"),
        P("dom", None, None, None),
        P("dom", None),
        P("dom"),
        P("dom"),
        P("dom", None),
    )
    out_specs = (P("feat", None), P(None, "feat"))
    return jax.shard_map(body, mesh=mesh, in_specs=in_specs, out_specs=out_specs, check_vma=False)
```

```python
import jax
import jax.numpy as jnp
from jax import lax
from jax.experimental import pallas as pl
from jax.experimental.pallas import tpu as pltpu
from jax.sharding import PartitionSpec as P

MESH = pl.DeviceIdType.MESH
BF16 = jnp.bfloat16
F32 = jnp.float32

NY = 8
NZC = 16
NZ = 8
NX = 4
PHASES = 12
FAR_8 = (4, 3, 5, 2, 6, 1, 7)
FAR_16 = (8, 7, 9, 6, 10, 5, 11, 4, 12, 3, 13, 2, 14, 1, 15)
FAR_4 = (2, 1, 3)


def dot(a, b):
    return lax.dot_general(a, b, (((1,), (0,)), ((), ())), preferred_element_type=F32)


def dot_nt(a, b):
    return lax.dot_general(a, b, (((1,), (1,)), ((), ())), preferred_element_type=F32)


def rows_of(ref, start, size):
    return ref.at[pl.ds(pl.multiple_of(start, size), size)]


def kernel(
    ft_hbm, pa_hbm, gt_hbm, wt_hbm, adj_hbm, cols_hbm, live_hbm, hc_hbm, br_hbm,
    out_ref,
    ft, pa, gt, wt, adj, hc, br, cols_ref, live_ref,
    amat, s0, r0, t0, u0, s1, r1, wall, sall, oall, t1s, su,
    q0s, q1s, q0, q1, w0, w1, v0, v1, f0, f1,
    load_sem, send_sem, recv_sem, ready_sem,
):
    dom = lax.axis_index("dom")
    feat = lax.axis_index("feat")
    y = dom // NZC
    zc = dom % NZC
    z = zc // 2
    core = dom % 2
    yc = y * 2 + core

    def dom_y(k):
        return ((y + k) % NY) * NZC + zc

    def dom_zc(k):
        return y * NZC + (zc + k) % NZC

    def place(j, own, size):
        return j + (j + size - own) // size

    barrier = pltpu.get_barrier_semaphore()

    def greet(d, f):
        pl.semaphore_signal(barrier, inc=1, device_id=(d, f), device_id_type=MESH)

    for k in FAR_16:
        greet(dom_zc(k), feat)
    for k in FAR_8:
        greet(dom_y(k), feat)
        greet(((y + k) % NY) * NZC + z * 2 + (1 - core), feat)
    for k in FAR_4:
        greet(dom, (feat + k) % NX)
    loads = []
    for i, (src, dst) in enumerate(
        [(br_hbm, br), (adj_hbm, adj), (ft_hbm, ft), (hc_hbm, hc), (gt_hbm, gt), (wt_hbm, wt), (pa_hbm, pa), (cols_hbm, cols_ref), (live_hbm, live_ref)]
    ):
        copy = pltpu.make_async_copy(src, dst, load_sem.at[i])
        copy.start()
        loads.append(copy)
    ld_br, ld_adj, ld_ft, ld_hc, ld_gt, ld_wt, ld_pa, ld_cols, ld_live = loads

    partners = (NY - 1) * 2 + (NZC - 1) + (NX - 1)

    def send(phase, src, dst, device):
        copy = pltpu.make_async_remote_copy(
            src_ref=src,
            dst_ref=dst,
            send_sem=send_sem.at[phase],
            recv_sem=recv_sem.at[phase],
            device_id=device,
            device_id_type=MESH,
        )
        copy.start()

    def scatter_y(phase, src, dst, rows):
        for k in FAR_8:
            send(phase, rows_of(src, ((y + k) % NY) * rows, rows), rows_of(dst, y * rows, rows), (dom_y(k), feat))
        rows_of(dst, y * rows, rows)[...] = rows_of(src, y * rows, rows)[...]

    def scatter_zc(phase, src, dst, rows):
        for k in FAR_16:
            send(phase, rows_of(src, ((zc + k) % NZC) * rows, rows), rows_of(dst, zc * rows, rows), (dom_zc(k), feat))
        rows_of(dst, zc * rows, rows)[...] = rows_of(src, zc * rows, rows)[...]

    def all_of(phase, ref, rows):
        return pltpu.make_async_remote_copy(
            src_ref=ref.at[pl.ds(0, rows)],
            dst_ref=ref.at[pl.ds(0, rows)],
            send_sem=send_sem.at[phase],
            recv_sem=recv_sem.at[phase],
            device_id=(dom_y(1), feat),
            device_id_type=MESH,
        )

    sent = []

    def arrive(phase, ref, rows):
        copies = all_of(phase, ref, rows)
        copies.wait_recv()
        sent.append(copies)

    n = 256
    rows_i = lax.broadcasted_iota(jnp.int32, (n, n), 0)
    lanes_i = lax.broadcasted_iota(jnp.int32, (n, n), 1)
    one_hot = lambda cond: jnp.where(cond, 1.0, 0.0).astype(BF16)
    eye = one_hot(rows_i == lanes_i)
    perm = one_hot(lanes_i == ((rows_i >> 1) & 7) * 32 + (rows_i >> 4) * 2 + (rows_i & 1))
    perm_p = one_hot(lanes_i == (rows_i & 15) * 16 + ((rows_i >> 4) & 7) * 2 + (rows_i >> 7))
    by_c = one_hot(lanes_i == (rows_i & 127) * 2 + (rows_i >> 7))
    eye128 = one_hot(
        lax.broadcasted_iota(jnp.int32, (128, 128), 0) == lax.broadcasted_iota(jnp.int32, (128, 128), 1)
    )
    peer_i = lax.broadcasted_iota(jnp.int32, (128, n), 0)
    slot_i = lax.broadcasted_iota(jnp.int32, (128, n), 1)
    even = one_hot(slot_i == 2 * peer_i)
    odd = one_hot(slot_i == 2 * peer_i + 1)

    ld_br.wait()
    border = br[...].astype(F32).astype(BF16)
    slot_row = dot(jnp.broadcast_to(border[0:1], (16, 128)), even) + dot(
        jnp.broadcast_to(border[1:2], (16, 128)), odd
    )
    hot_t = one_hot(rows_i.astype(F32) == slot_row[0:1])
    hot = dot_nt(eye, hot_t).astype(BF16)
    hot_c = dot_nt(by_c, hot_t).astype(BF16)

    ld_ft.wait()
    s0[...] = dot_nt(hot, jnp.concatenate([ft[...], jnp.zeros((64, n), BF16)], axis=0)).astype(BF16)

    ld_hc.wait()
    counts = jnp.broadcast_to(hc[...].astype(F32).astype(BF16), (16, 128))
    slot_counts = dot(counts, even + odd)[0:1]
    parity = (lax.broadcasted_iota(jnp.int32, (1, n), 1) & 1).astype(F32)
    flags = jnp.where(parity < slot_counts, 1.0, 0.0)
    ld_cols.wait()
    ld_live.wait()
    ld_adj.wait()
    for b in range(2):
        for cb in range(4):
            total = jnp.zeros((128, 128), jnp.int32)
            for s in range(6):
                keep = jnp.logical_and(cols_ref[b, s] == cb, s < live_ref[b])
                total = total + (adj[b, s] & jnp.where(keep, -1, 0))
            total = total.astype(F32)
            if cb >= 2:
                total = total * flags[:, (cb - 2) * 128 : (cb - 1) * 128]
            amat[b * 128 : (b + 1) * 128, cb * 128 : (cb + 1) * 128] = total.astype(BF16)
    inverse = 1.0 / dot_nt(jnp.ones((16, 512), BF16), amat[...])[0:1]

    ld_gt.wait()
    scaled = gt[...].astype(F32) * inverse
    high = scaled.astype(BF16)
    low = (scaled - high.astype(F32)).astype(BF16)
    spread = dot(jnp.concatenate([high, low], axis=0), amat[...])
    spread = spread[0:64] + spread[64:128]
    own_part = spread[:, 0:256]
    halo_part = spread[:, 256:512].astype(BF16)
    s1[...] = dot_nt(perm, jnp.concatenate([halo_part, halo_part], axis=0)).astype(BF16)

    pl.semaphore_wait(barrier, partners)
    scatter_zc(2, s1, r1, 16)
    for k in FAR_8:
        pl.semaphore_signal(ready_sem, inc=1, device_id=(dom_y(k), feat), device_id_type=MESH)
    scatter_y(0, s0, r0, 32)
    ld_wt.wait()
    for k in FAR_4:
        send(4, wt, rows_of(wall, feat * 64, 64), (dom, (feat + k) % NX))
    rows_of(wall, feat * 64, 64)[...] = wt[...]

    rows_of(oall, feat * 64, 64)[...] = own_part.astype(BF16)
    for k in FAR_4:
        send(5, rows_of(oall, feat * 64, 64), rows_of(oall, feat * 64, 64), (dom, (feat + k) % NX))

    a_own = amat[:, 0:256]
    a_halo = amat[:, 256:512]
    a_halo_p = dot_nt(a_halo, perm).astype(BF16)
    mixed = dot_nt(ft[...], a_own)
    ld_pa.wait()
    pre = pa[...].astype(F32)
    act = jnp.maximum(pre, 0.0).astype(BF16)
    mask_t = dot_nt(eye, one_hot(pre > 0.0))

    arrive(2, r1, 240)
    pl.semaphore_wait(ready_sem, NY - 1)
    packed = dot(perm_p, r1[...])
    t1s[...] = jnp.where(
        lax.broadcasted_iota(jnp.int32, (128, 128), 1) < 64, packed[0:128], packed[128:256]
    ).astype(BF16)
    for k in FAR_8 + (0,):
        for m in FAR_4 + (0,):
            if k + m > 0:
                send(
                    3,
                    rows_of(t1s, ((y + k) % NY) * 16, 16),
                    rows_of(su, feat * 128 + y * 16, 16),
                    (dom_y(k), (feat + m) % NX),
                )
    rows_of(su, feat * 128 + y * 16, 16)[...] = rows_of(t1s, y * 16, 16)[...]
    arrive(0, r0, 224)
    t0[...] = dot(perm, r0[...]).astype(BF16)
    scatter_zc(1, t0, u0, 16)

    arrive(5, oall, 192)
    own_all = oall[...].astype(F32)
    arrive(4, wall, 192)
    w_full = dot_nt(eye, wall[...]).astype(BF16)

    arrive(3, su, 496)
    x_s = dot_nt(eye128, su[...]).astype(BF16)
    even_part = jnp.concatenate([x_s[0:64, i * 128 : (i + 1) * 128] for i in range(NX)], axis=0)
    odd_part = jnp.concatenate([x_s[64:128, i * 128 : (i + 1) * 128] for i in range(NX)], axis=0)
    gathered = own_all + dot(jnp.concatenate([even_part, odd_part], axis=1), hot_c)
    sall[...] = gathered.astype(BF16)

    arrive(1, u0, 240)
    x0 = dot_nt(eye, u0[...]).astype(BF16)
    mixed_in = ((mixed + dot_nt(x0[0:192], a_halo_p)) * inverse).astype(BF16)

    second = dot(rows_of(sall, feat * 64, 64)[...], act)
    q0s[192:256] = second[:, 0:128].astype(BF16)
    q1s[192:256] = second[:, 128:256].astype(BF16)
    grad_act = dot(w_full, sall[...])
    grad_pre = jnp.where(mask_t > 0.5, grad_act, 0.0).astype(BF16)
    first = dot_nt(mixed_in, grad_pre)
    q0s[0:192] = first[:, 0:128].astype(BF16)
    q1s[0:192] = first[:, 128:256].astype(BF16)

    on_y = lambda k: (((y + k) % NY) * NZC + z * 2 + 1, feat)
    on_z = lambda k: (y * NZC + ((z + k) % NZ) * 2 + 1, feat)

    def scatter_to_owner(k):
        send(6, rows_of(q0s, ((y + k) % NY) * 32, 32), rows_of(q0, yc * 32, 32), on_y(k))
        send(7, rows_of(q1s, ((z + k) % NZ) * 32, 32), rows_of(q1, zc * 32, 32), on_z(k))

    for k in FAR_8:
        scatter_to_owner(k)

    def total_of(ref, members):
        total = ref[0:32].astype(F32)
        for i in range(1, members):
            total = total + ref[i * 32 : (i + 1) * 32].astype(F32)
        return total.astype(BF16)

    @pl.when(core == 0)
    def _():
        scatter_to_owner(0)
        all_of(10, out_ref, 256).wait_recv()
        all_of(11, out_ref, 256).wait_recv()
        all_of(6, q0, 256).wait_send()
        all_of(7, q1, 256).wait_send()

    @pl.when(core == 1)
    def _():
        rows_of(q0, yc * 32, 32)[...] = rows_of(q0s, y * 32, 32)[...]
        rows_of(q1, zc * 32, 32)[...] = rows_of(q1s, z * 32, 32)[...]
        all_of(6, q0, 480).wait_recv()
        part0 = total_of(q0, 16)
        w0[...] = part0
        for k in FAR_8:
            send(8, w0, rows_of(v0, z * 32, 32), on_z(k))
        rows_of(v0, z * 32, 32)[...] = part0
        all_of(7, q1, 480).wait_recv()
        part1 = total_of(q1, 16)
        w1[...] = part1
        for k in FAR_8:
            send(9, w1, rows_of(v1, y * 32, 32), (dom_y(k), feat))
        rows_of(v1, y * 32, 32)[...] = part1

        all_of(8, v0, 224).wait_recv()
        f0[...] = total_of(v0, 8)
        for k in FAR_8:
            send(10, f0, rows_of(out_ref, y * 32, 32), (dom_y(k), feat))
        for k in FAR_8 + (0,):
            send(10, f0, rows_of(out_ref, y * 32, 32), (dom_y(k) - 1, feat))
        own0 = pltpu.make_async_copy(f0, rows_of(out_ref, y * 32, 32), load_sem.at[9])
        own0.start()
        all_of(9, v1, 224).wait_recv()
        f1[...] = total_of(v1, 8)
        for k in FAR_8:
            send(11, f1, rows_of(out_ref, 256 + z * 32, 32), on_z(k))
        for k in FAR_8 + (0,):
            send(11, f1, rows_of(out_ref, 256 + z * 32, 32), (on_z(k)[0] - 1, feat))
        own1 = pltpu.make_async_copy(f1, rows_of(out_ref, 256 + z * 32, 32), load_sem.at[10])
        own1.start()
        own0.wait()
        own1.wait()
        all_of(10, out_ref, 224).wait_recv()
        all_of(11, out_ref, 224).wait_recv()
        all_of(6, q0, 224).wait_send()
        all_of(7, q1, 224).wait_send()
        all_of(8, v0, 224).wait_send()
        all_of(9, v1, 224).wait_send()
        all_of(10, q0, 480).wait_send()
        all_of(11, q1, 480).wait_send()

    for copies in sent:
        copies.wait_send()


def widen(sums, first_ref, second_ref):
    for h in range(2):
        first_ref[:, h * 128 : (h + 1) * 128] = sums[h * 256 : h * 256 + 192].astype(F32)
        second_ref[:, h * 128 : (h + 1) * 128] = sums[h * 256 + 192 : h * 256 + 256].astype(F32)


def body(
    features, pre_act, out_grad, w_second, adj_tiles, tile_cols, tile_live, halo_counts, border_rows
):
    anywhere = pl.BlockSpec(memory_space=pl.ANY)
    vmem = pl.BlockSpec(memory_space=pltpu.VMEM)
    half = pltpu.VMEM((256, 128), BF16)
    square = pltpu.VMEM((256, 256), BF16)
    grads = pl.pallas_call(
        kernel,
        out_shape=pltpu.VMEM((512, 128), BF16),
        in_specs=[anywhere] * 9,
        out_specs=anywhere,
        scratch_shapes=[
            pltpu.VMEM((192, 256), BF16),
            square,
            pltpu.VMEM((64, 256), BF16),
            pltpu.VMEM((64, 256), BF16),
            pltpu.VMEM((2, 6, 128, 128), jnp.int32),
            pltpu.VMEM((1, 128), jnp.int32),
            pltpu.VMEM((2, 128), jnp.int32),
            pltpu.SMEM((2, 6), jnp.int32),
            pltpu.SMEM((2,), jnp.int32),
            pltpu.VMEM((256, 512), BF16),
            square, square, square, square, half, half,
            square, square, square,
            pltpu.VMEM((128, 128), BF16),
            pltpu.VMEM((512, 128), BF16),
            half, half,
            pltpu.VMEM((512, 128), BF16),
            pltpu.VMEM((512, 128), BF16),
            pltpu.VMEM((32, 128), BF16), pltpu.VMEM((32, 128), BF16), half, half, pltpu.VMEM((32, 128), BF16), pltpu.VMEM((32, 128), BF16),
            pltpu.SemaphoreType.DMA((11,)),
            pltpu.SemaphoreType.DMA((PHASES,)),
            pltpu.SemaphoreType.DMA((PHASES,)),
            pltpu.SemaphoreType.REGULAR,
        ],
        compiler_params=pltpu.CompilerParams(collective_id=0, has_side_effects=True, vmem_limit_bytes=60 * 1024 * 1024),
        name="sage_backward",
    )(
        features.T, pre_act, out_grad.T, w_second.T, adj_tiles, tile_cols, tile_live,
        halo_counts.reshape(1, 128), border_rows.T,
    )
    grad_first, grad_second_t = pl.pallas_call(
        widen,
        out_shape=(
            jax.ShapeDtypeStruct((192, 256), F32),
            jax.ShapeDtypeStruct((64, 256), F32),
        ),
        in_specs=[vmem],
        out_specs=(vmem, vmem),
        compiler_params=pltpu.CompilerParams(vmem_limit_bytes=4 * 1024 * 1024),
        name="widen",
    )(grads)
    return grad_first, grad_second_t.T


def solution(mesh):
    in_specs = (
        P("dom", "feat"),
        P("dom", None),
        P("dom", "feat"),
        P(None, "feat"),
        P("dom", None, None, None),
        P("dom", None),
        P("dom"),
        P("dom"),
        P("dom", None),
    )
    out_specs = (P("feat", None), P(None, "feat"))
    return jax.shard_map(body, mesh=mesh, in_specs=in_specs, out_specs=out_specs, check_vma=False)
```
